256 devices in a mesh: rep: 8 (over y, core), grp: 32 (over x, z).
Axes of the slice: x: 4, y: 4, z: 8, core: 2. Of those that a mesh axis runs over, the one named last changes fastest.
Arguments:
- grad_parts: bfloat16 [8, 32, 256, 8192], P('rep', 'grp'), may hold values from -180 to 180
- stats: float32 [128, 2, 256, 256], P('grp'), may hold values from -0.2 to 34, as said below
- owner: int32 [32], replicated, may hold values from 0 to 31, as said below
Outputs:
- direction: float32 [256, 8192], P('grp')
- new_stats: float32 [128, 2, 256, 256], P('grp')
The draws below stay inside these ranges and needn't reach their ends.
Inputs may be any that keep to these rules, and one draw needn't show every extreme that they name: `stats`: each left and right statistic is symmetric with a positive diagonal that exceeds the sum of magnitudes off the diagonal in its row. `owner`: no device owns more than 4 blocks, and some device owns exactly 4.
All inputs are finite; a program needn't handle non-finite values.
Results may differ from the reference program's by a relative error of at most 0.0003.
Values may be sent and summed in bfloat16 or wider, within the bound.
A program may use at most 128 MiB of HBM per device.

```python
import math
import jax
import jax.numpy as jnp
from jax import lax

D = 8192
ROWS = 256
BS = 256
ITERS = 6
NB = 32
M = 4
N_REP = 8
N_GRP = 32


def draw_grad_parts(key, part):
    key = jax.random.fold_in(key, 11)
    key_rows, key_cols, key_noise = jax.random.split(key, 3)
    row_scale = jnp.exp(jax.random.uniform(key_rows, (ROWS, 1), jnp.float32, math.log(0.4), math.log(4.0)))
    col_scale = jnp.exp(jax.random.uniform(key_cols, (1, D), jnp.float32, math.log(0.4), math.log(4.0)))
    noise = jnp.clip(jax.random.normal(key_noise, (N_REP, N_GRP, ROWS, D), jnp.float32), -5.0, 5.0)
    values = noise * (row_scale * col_scale)
    return values.astype(jnp.bfloat16)


def draw_stats(key, part):
    key = jax.random.fold_in(key, 23)
    key_scale, key_diag, key_off = jax.random.split(key, 3)
    total_slots = N_GRP * M
    shape = (total_slots, 2, BS, BS)
    ramp = (jnp.arange(total_slots, dtype=jnp.float32) / (total_slots - 1)).reshape(total_slots, 1, 1, 1)
    jitter = jnp.exp(jax.random.uniform(key_scale, (total_slots, 2, 1, 1), jnp.float32, math.log(0.7), math.log(1.4)))
    uniform_diag = jax.random.uniform(key_diag, (total_slots, 2, BS), jnp.float32, 0.0, 1.0)
    diag_part = 1.0 + uniform_diag
    block_scale = jnp.exp(math.log(0.3) + ramp * math.log(10.0)) * jitter
    raw_off = jax.random.uniform(key_off, shape, jnp.float32, -1.0, 1.0)
    symmetric = (raw_off + jnp.swapaxes(raw_off, -1, -2)) * 0.5
    identity = jnp.eye(BS, dtype=jnp.float32)
    off_part = symmetric * (1.0 - identity) * (0.9 / (BS - 1))
    return ((off_part + identity * diag_part[..., None]) * block_scale).astype(jnp.float32)


def draw_owner(key, part):
    key = jax.random.fold_in(key, 37)
    key_first, key_slots, key_blocks = jax.random.split(key, 3)
    total_slots = N_GRP * M
    first_owner = jax.random.randint(key_first, (), 0, N_GRP)
    shuffled = jax.random.permutation(key_slots, total_slots)
    position = jnp.argsort(shuffled)
    slot_owner = jnp.arange(total_slots) // M
    score = jnp.where(slot_owner == first_owner, 0, total_slots) + position
    chosen = jnp.argsort(score)[:NB]
    return jax.random.permutation(key_blocks, chosen // M).astype(jnp.int32)


def setup_inputs(seed: int = 0) -> dict:
    seeds = jax.random.split(jax.random.key(seed), 4)
    return {
        "grad_parts": draw_grad_parts(jax.random.fold_in(seeds[3], 71), 0),
        "stats": draw_stats(jax.random.fold_in(seeds[3], 71), 0),
        "owner": draw_owner(jax.random.fold_in(seeds[3], 71), 0),
    }


decay_rate = 0.9

def exact_dot(left_mat, right_mat):
    return jnp.matmul(left_mat, right_mat, precision=lax.Precision.HIGHEST)

def inverse_root(matrix):
    size = matrix.shape[-1]
    identity = jnp.eye(size, dtype=jnp.float32)
    norm_value = jnp.sqrt(lax.optimization_barrier(jnp.sum(matrix * matrix, axis=(-2, -1), keepdims=True)))
    result = identity * norm_value ** (-0.25)
    normalized = matrix / norm_value
    for iteration in range(ITERS):
        factor = (5.0 * identity - normalized) * 0.25
        result = exact_dot(result, factor)
        square = exact_dot(factor, factor)
        normalized = exact_dot(exact_dot(square, square), normalized)
    return result

def reference(grad_parts, stats, owner):
    flat_parts = grad_parts.reshape(N_REP * N_GRP, ROWS, D)

    def accumulate(total, partial_value):
        return (total + partial_value.astype(jnp.float32), None)
    total, _ = lax.scan(accumulate, jnp.zeros((ROWS, D), jnp.float32), flat_parts)
    grad = total / (N_REP * N_GRP)
    blocks = grad.reshape(ROWS // BS, BS, D // BS, BS).transpose(0, 2, 1, 3).reshape(NB, BS, BS)
    block_ids = jnp.arange(NB, dtype=jnp.int32)
    same_owner = owner[:, None] == owner[None, :]
    earlier = block_ids[:, None] > block_ids[None, :]
    block_rank = lax.optimization_barrier(jnp.sum((same_owner & earlier).astype(jnp.int32), axis=1)).astype(jnp.int32)
    slot = (owner * M + block_rank).astype(jnp.int32)
    old_pairs = jnp.take(stats, slot, axis=0)

    def per_block(inputs):
        block, old_pair = inputs
        left_stat = decay_rate * old_pair[0] + exact_dot(block, block.T)
        right_stat = decay_rate * old_pair[1] + exact_dot(block.T, block)
        stat_pair = jnp.stack([left_stat, right_stat])
        root_pair = inverse_root(stat_pair)
        precond = exact_dot(exact_dot(root_pair[0], block), root_pair[1])
        return (precond, stat_pair)
    precond, stat_pairs = lax.map(per_block, (blocks, old_pairs))
    graft_ratio = jnp.sqrt(jnp.sum(blocks * blocks) / jnp.sum(precond * precond))
    scaled = precond * graft_ratio
    direction = scaled.reshape(ROWS // BS, D // BS, BS, BS).transpose(0, 2, 1, 3).reshape(ROWS, D)
    new_stats = stats.at[slot].set(stat_pairs)
    return (direction, new_stats)
```

```python
import functools
import jax
import jax.numpy as jnp
from jax import lax
from jax.experimental import pallas as pl
from jax.experimental.pallas import tpu as pltpu
from jax.sharding import PartitionSpec as P

BS = 256
ITERS = 6
DECAY = 0.9
NX, NY, NZ, NC = 4, 4, 8, 2
NB, SLOTS = 32, 4
MESH = pl.DeviceIdType.MESH
F32, BF16, I16 = jnp.float32, jnp.bfloat16, jnp.int16
TOP = 32700.0


def split(a):
    hi = a.astype(BF16)
    return hi, (a - hi.astype(F32)).astype(BF16)


def dot3(a, b):
    rows = a[0].shape[0]
    both = jnp.dot(jnp.concatenate(a, axis=0), b[0], preferred_element_type=F32)
    return both[:rows] + (both[rows:] + jnp.dot(a[0], b[1], preferred_element_type=F32))


def scale_of(code):
    return jnp.exp2(code * 0.125) * (1.0 / TOP)


def code_of(top):
    return jnp.ceil(jnp.log2(jnp.maximum(top, 1e-30)) * 8.0)


def rounded(v, inverse):
    q = (v * inverse + 12582912.0) - 12582912.0
    return to16(q.reshape(v.shape[0] * 8, 128))


def peak(v):
    return jnp.max(jnp.abs(v), axis=0)


def narrow(v):
    code = code_of(jnp.max(peak(v), axis=0, keepdims=True))
    return rounded(v, 1.0 / scale_of(code)), code


def to16(v):
    return v.astype(jnp.int32).astype(I16)


def wide(q):
    return q.astype(jnp.int32)


def sum_rows(v):
    v = jnp.maximum(v, 1e-36)
    e = jnp.floor(jnp.log2(v))
    return [e, jnp.round((v * jnp.exp2(-e) - 1.0) * 16000.0)]


def sums_from(rows):
    return jnp.exp2(rows[0:1]) * (1.0 + rows[1:2] * (1.0 / 16000.0))


def tail(rows):
    left = 16 - sum(r.shape[0] for r in rows)
    zero = [jnp.zeros((left, 128), F32)] if left else []
    return to16(jnp.concatenate(list(rows) + zero, axis=0))


def kernel(
    grad, stats_hbm, owner_hbm,
    fq, ratio_ref, ns,
    stats, own, sib,
    m1, rm1, red, m2, rm2, s_buf, m3, rm3, c3, rc3, gx0, gx1, gc0, gc1, m5, rm5, c5, rc5, gq, gbuf, codes, acc,
    xs, qs, xother, ma, rma, my, rmy,
    owner, rank, local_j,
    s_owner, s_own, s_stat, s_sib, r_sib, s_1, r_1, s_2, r_2, s_3, r_3, s_4, r_4, s_5, r_5,
    s_d, r_d, s_6, r_6, s_7, r_7, s_x, r_x, s_a, r_a, s_y, r_y, s_ag, r_ag,
):
    gx, gc = (gx0, gx1), (gc0, gc1)
    rep, grp = lax.axis_index("rep"), lax.axis_index("grp")
    y, c = lax.div(rep, 2), lax.rem(rep, 2)
    x, z = lax.div(grp, 8), lax.rem(grp, 8)

    def wrap(v, n):
        return lax.rem(v + n, n)

    def dev(dy=0, dc=0, dx=0, dz=0):
        return (wrap(y + dy, NY) * 2 + wrap(c + dc, 2), wrap(x + dx, NX) * 8 + wrap(z + dz, NZ))

    pending = []

    def remote(src, dst, ssem, rsem, to):
        return pltpu.make_async_remote_copy(
            src_ref=src, dst_ref=dst, send_sem=ssem, recv_sem=rsem, device_id=to, device_id_type=MESH
        )

    def send(src, dst, ssem, rsem, to):
        copy = remote(src, dst, ssem, rsem, to)
        copy.start()
        pending.append(copy)
        return copy

    def flush():
        for q in pending:
            q.wait_send()
        pending.clear()

    def xcols(k):
        return pl.ds(pl.multiple_of(wrap(x + k, NX) * 1024, 1024), 1024)

    def chunk(axis, k, h, core=None):
        lead = () if core is None else (core,)
        if axis == 0:
            yy = pl.ds(0, 4) if h is None else pl.ds(2 * h, 2)
            return (yy,) + lead + (slice(None), xcols(k))
        cols = pl.ds(4096, 4096) if h is None else pl.ds(4096 + 2048 * h, 2048)
        return (wrap(y + k, NY),) + lead + (slice(None), cols)

    pieces_in_order = [(axis, k, h) for k, h in ((2, 0), (2, 1), (1, None), (-1, None), (0, None)) for axis in range(2)]
    def own_copy(i, axis, k, h):
        return pltpu.make_async_copy(grad.at[chunk(axis, k, h, c)], own.at[chunk(axis, k, h)], s_own.at[i])

    for i, piece in enumerate(pieces_in_order):
        own_copy(i, *piece).start()
    owner_copy = pltpu.make_async_copy(owner_hbm, owner, s_owner)
    owner_copy.start()
    stat_copy = pltpu.make_async_copy(stats_hbm, stats, s_stat)
    stat_copy.start()

    partners = [dict(dc=1)]
    partners += [dict(dx=j) for j in (1, -1, 2)] + [dict(dy=i) for i in (1, -1, 2)]
    partners += [dict(dz=k) for k in range(1, NZ)]
    barrier = pltpu.get_barrier_semaphore()
    for p in partners:
        pl.semaphore_signal(barrier, inc=1, device_id=dev(**p), device_id_type=MESH)
    pl.semaphore_wait(barrier, len(partners))

    oc = wrap(c + 1, 2)
    def sib_copy(i, axis, k, h):
        return remote(grad.at[chunk(axis, k, h, oc)], sib.at[chunk(axis, k, h)], s_sib.at[i], r_sib.at[i], dev(dc=1))

    def begin(copies):
        for q in copies:
            q.start()
            pending.append(q)

    for i, piece in enumerate(pieces_in_order):
        begin([sib_copy(i, *piece)])

    def ready(i, axis, k, h):
        own_copy(i, axis, k, h).wait()
        sib_copy(i, axis, k, h).wait_recv()

    def tile(v):
        return v.reshape(4, 8, 128)

    def unit(axis, k, h, a, b):
        if axis == 0:
            row, at = 2 * h + a, wrap(x + k, NX) * 1024 + b * 128
        else:
            row, at = wrap(y + k, NY), 4096 + 2048 * h + (a * 8 + b) * 128
        at = pl.ds(pl.multiple_of(at, 128), 128)
        return own[row, :, at].astype(F32) + sib[row, :, at].astype(F32)

    def unit_rows(n):
        return pl.ds(n * 32 if isinstance(n, int) else pl.multiple_of(n * 32, 32), 32)

    def scale_tile(rows):
        return scale_of(wide(rows).astype(F32)[0:8])

    def scale_tile(rows):
        return scale_of(wide(rows).astype(F32)[0:8])

    def part(u, axis, k, h, adds, flow):
        scales = [scale_tile(rm1[u, axis, f, pl.ds(256, 16)]) for f in adds]
        zero = jnp.zeros((8, 128), F32)
        tops = [zero, zero]
        for a in range(2):
            for i in range(4):
                v = tile(unit(axis, k, h, a, 2 * i + u))
                for f, scale in zip(adds, scales):
                    v = v + tile(wide(rm1[u, axis, f, unit_rows(4 * a + i)]).astype(F32)) * scale
                if flow is None:
                    red[u, axis, 2 * h + a, i] = v
                else:
                    acc[a, i] = v
                tops[a] = jnp.maximum(tops[a], peak(v))
        if flow is not None:
            tops = [jnp.maximum(tops[0], tops[1])] * 2
        codes = [code_of(t) for t in tops]
        inverse = [1.0 / scale_of(code) for code in codes]
        for a in range(2):
            for i in range(4):
                if flow is None:
                    m2[u, axis, 2 * h + a, unit_rows(i)] = rounded(red[u, axis, 2 * h + a, i], inverse[a])
                else:
                    m1[u, axis, flow, unit_rows(4 * a + i)] = rounded(acc[a, i], inverse[a])
            if flow is None:
                m2[u, axis, 2 * h + a, pl.ds(128, 16)] = tail([codes[a]])
        if flow is not None:
            m1[u, axis, flow, pl.ds(256, 16)] = tail([codes[0]])

    def flow_copy(u, axis, f, hop):
        to = dev(dx=hop) if axis == 0 else dev(dy=hop)
        return remote(m1.at[u, axis, f], rm1.at[u, axis, f], s_1.at[u, axis, f], r_1.at[u, axis, f], to)

    def arrived(u, axis, f):
        flow_copy(u, axis, f, 1).wait_recv()

    def far(u):
        def body(h, carry):
            for axis in range(2):
                if u == 0:
                    ready(2 * h + axis, axis, 2, h)
                part(u, axis, 2, h, [], h)
                flow_copy(u, axis, h, 1 - 2 * h).start()
            return carry

        lax.fori_loop(0, 2, body, 0)

    def near(u):
        def body(h, carry):
            hop = 2 * h - 1
            for axis in range(2):
                if u == 0:
                    ready(6 - 2 * h + axis, axis, hop, None)
                part(u, axis, hop, h, [], 2 + h)
                flow_copy(u, axis, 2 + h, hop).start()
            return carry

        lax.fori_loop(0, 2, body, 0)

    def onward(u):
        def body(h, carry):
            hop = 1 - 2 * h
            for axis in range(2):
                arrived(u, axis, h)
                part(u, axis, hop, h, [h], 4 + h)
                flow_copy(u, axis, 4 + h, hop).start()
            return carry

        lax.fori_loop(0, 2, body, 0)
        for axis in range(2):
            for f in range(6):
                pending.append(flow_copy(u, axis, f, 1))

    def p2_copy(u, axis, to, at, frm):
        return remote(m2.at[u, axis, to], rm2.at[u, axis, frm], s_2.at[u, axis, to], r_2.at[u, axis, frm], at)

    def p2_send(u, axis, to):
        me = (y, x)[axis]
        at = dev(dy=to - y) if axis == 0 else dev(dx=to - x)

        @pl.when(me != to)
        def _():
            p2_copy(u, axis, to, at, me).start()

    def last(u):
        def body(h, carry):
            for axis in range(2):
                arrived(u, axis, 2 + h)
                arrived(u, axis, 4 + h)
                part(u, axis, 0, h, [2 + h, 4 + h], None)
                p2_send(u, axis, 2 * h)
                p2_send(u, axis, 2 * h + 1)
            return carry

        if u == 0:
            for axis in range(2):
                ready(8 + axis, axis, 0, None)
        lax.fori_loop(0, 2, body, 0)

    def p3_copies(u, to, at, frm):
        return (remote(c3.at[u, to], rc3.at[u, frm], s_3.at[u, 0, to], r_3.at[u, 0, frm], at),
                remote(m3.at[u, to], rm3.at[u, frm], s_3.at[u, 1, to], r_3.at[u, 1, frm], at))

    def column_code(v):
        return code_of(jnp.max(peak(v), axis=0, keepdims=True))

    def along_z(u):
        scales = {}
        for axis in range(2):
            me = (y, x)[axis]
            for k in range(1, 4):
                frm = wrap(me - k, 4)
                q = p2_copy(u, axis, wrap(me + k, 4), dev(dc=1), frm)
                pending.append(q)
                q.wait_recv()
                scales[axis, k] = scale_tile(rm2[u, axis, frm, pl.ds(128, 16)])

        def sum2(j, carry):
            for axis in range(2):
                me = (y, x)[axis]
                v = red[u, axis, me, j]
                for k in range(1, 4):
                    v = v + tile(wide(rm2[u, axis, wrap(me - k, 4), unit_rows(j)]).astype(F32)) * scales[axis, k]
                to = 4 * axis + j
                s_buf[u, to] = v
                code = column_code(v)
                c3[u, to] = code
                m3[u, to] = rounded(v, 1.0 / scale_of(code))

                @pl.when(z != to)
                def _():
                    for q in p3_copies(u, to, dev(dz=to - z), z):
                        q.start()

            return carry

        lax.fori_loop(0, 4, sum2, 0)

    def p4_copies(u, src, k):
        return (remote(gc[u].at[src], gc[u].at[src], s_4.at[u, 0, k - 1], r_4.at[u, 0, k - 1], dev(dz=k)),
                remote(gx[u].at[src], gx[u].at[src], s_4.at[u, 1, k - 1], r_4.at[u, 1, k - 1], dev(dz=k)))

    def gather_z(u):
        piece = s_buf[u, z]
        for k in range(1, NZ):
            for q in p3_copies(u, wrap(z + k, NZ), dev(dc=1), wrap(z - k, NZ)):
                pending.append(q)
                q.wait_recv()
        for k in range(1, NZ):
            frm = wrap(z - k, NZ)
            piece = piece + tile(wide(rm3[u, frm]).astype(F32)) * scale_of(rc3[u, frm])
        piece = piece * (1.0 / 256.0)
        code = column_code(piece)
        gc[u][z] = code
        gx[u][z] = rounded(piece, 1.0 / scale_of(code))
        for k in (4, 3, 5, 2, 6, 1, 7):
            begin(p4_copies(u, z, k))
        return piece

    def p5_copies(u, e):
        at = dev(dy=e // 4, dx=e % 4)
        return (remote(c5.at[u, e], rc5.at[u, e], s_5.at[u, 0, e], r_5.at[u, 0, e], at),
                remote(m5.at[u, e], rm5.at[u, e], s_5.at[u, 1, e], r_5.at[u, 1, e], at))

    def route(u):
        for k in range(1, NZ):
            for q in p4_copies(u, wrap(z - k, NZ), k):
                q.wait_recv()
        for i in (2, 1, 3, 0):
            for j in (2, 1, 3, 0):
                e = i * 4 + j
                which = local_j[wrap(x + j, NX) * SLOTS + wrap(y + i, NY)]
                take = jnp.maximum(which, 0)
                c5[u, e] = jnp.where(which >= 0, gc[u][take], jnp.zeros((1, 128), F32))
                m5[u, e] = jnp.where(which >= 0, wide(gx[u][take]), jnp.zeros((32, 128), jnp.int32)).astype(I16)
                if e:
                    begin(p5_copies(u, e))

    def half_copy(u, core):
        return remote(gq.at[y, core, u], gq.at[y, core, u], s_d.at[u], r_d.at[u], dev(dc=1))

    def open_half(slot, core, u):
        for i in range(NY):
            scale = scale_of(wide(gq[slot, core, u, i, pl.ds(32, 16)]).astype(F32)[0:1])
            v = tile(wide(gq[slot, core, u, i, pl.ds(0, 32)]).astype(F32)) * scale
            gbuf[i, core, :, pl.ds(u * 128, 128)] = v.reshape(32, 128)

    def collect(u):
        for i in range(NY):
            parts = [(m5[u, 0], c5[u, 0])] if i == 0 else []
            for j in range(NX):
                e = i * 4 + j
                if e:
                    for q in p5_copies(u, e):
                        q.wait_recv()
                    parts.append((rm5[u, e], rc5[u, e]))
            rows = [wide(v[0]) for v in parts]
            yi = wrap(y - i, NY)
            gq[y, c, u, yi, pl.ds(0, 32)] = ((rows[0] + rows[1]) + (rows[2] + rows[3])).astype(I16)
            code = (parts[0][1] + parts[1][1]) + (parts[2][1] + parts[3][1])
            gq[y, c, u, yi, pl.ds(32, 16)] = tail([code])
        begin([half_copy(u, c)])

    def rank_row(b, carry):
        ob = owner[b]
        total = jnp.int32(0)
        for e in range(NB):
            total = total + jnp.where((owner[e] == ob) & (e < b), 1, 0)
        rank[b] = total
        return carry

    def find(i, carry):
        target = lax.div(i, SLOTS) * NZ + z
        slot = lax.rem(i, SLOTS)
        found = jnp.int32(-1)
        for j in range(8):
            b = 4 * x + j if j < 4 else 16 + 4 * x + j - 4
            found = jnp.where((owner[b] == target) & (rank[b] == slot), j, found)
        local_j[i] = found
        return carry

    far(0)
    near(0)
    far(1)
    onward(0)
    near(1)
    onward(1)
    owner_copy.wait()
    lax.fori_loop(0, NB, rank_row, 0)
    last(0)
    last(1)
    along_z(0)
    along_z(1)
    lax.fori_loop(0, NX * SLOTS, find, 0)
    n_mine = jnp.int32(0)
    for b in range(NB):
        n_mine = n_mine + jnp.where(owner[b] == grp, 1, 0)
    pieces = [gather_z(u) for u in range(2)]
    route(0)
    route(1)
    collect(0)
    collect(1)
    g_square = jnp.sum(jnp.sum(pieces[0] * pieces[0] + pieces[1] * pieces[1], axis=0), axis=0, keepdims=True)

    def block_copies(slot, core, ssem, rsem, to):
        return [remote(gq.at[slot, core], gq.at[slot, core], ssem, rsem, to)]

    for k in (2, 1, 3):
        begin(block_copies(y, c, s_6.at[k - 1], r_6.at[k - 1], dev(dy=k)))
    stat_copy.wait()
    for u in range(2):
        open_half(y, c, u)
    for u in range(2):
        half_copy(u, oc).wait_recv()
        open_half(y, oc, u)

    def put_stats(slot, side, value):
        ns[slot, side] = jnp.where(n_mine > slot, value, stats[slot, side])

    def slot_stats(slot):
        for core in range(NC):
            for u in range(2):
                open_half(slot, core, u)
        g = gbuf[...].reshape(BS, BS)
        gp, gtp = split(g), split(g.T)
        put_stats(slot, 0, DECAY * stats[slot, 0] + dot3(gp, gtp))
        put_stats(slot, 1, DECAY * stats[slot, 1] + dot3(gtp, gp))

    g = gbuf[...].reshape(BS, BS)
    gt = g.T
    first, second = jnp.where(c == 0, g, gt), jnp.where(c == 0, gt, g)
    first_p, second_p = split(first), split(second)
    mat = DECAY * stats[y, c] + dot3(first_p, second_p)
    put_stats(y, c, mat)
    norm = jnp.sqrt(jnp.sum(jnp.sum(mat * mat, axis=0, keepdims=True), axis=1, keepdims=True))
    five = jnp.where(
        lax.broadcasted_iota(jnp.int32, (BS, BS), 0) == lax.broadcasted_iota(jnp.int32, (BS, BS), 1), 1.25, 0.0
    ).astype(F32)
    q0 = mat / norm
    factor = five - 0.25 * q0
    xs[...] = factor * lax.rsqrt(jnp.sqrt(norm))

    def advance(factor, q):
        fp = split(factor)
        square = split(dot3(fp, fp))
        return dot3(split(dot3(square, square)), split(q))

    qs[...] = advance(factor, q0)

    def newton(i, carry):
        q = qs[...]
        factor = five - 0.25 * q
        xs[...] = dot3(split(xs[...]), split(factor))
        qs[...] = advance(factor, q)
        return carry

    lax.fori_loop(0, ITERS - 3, newton, 0)
    q = qs[...]
    factor = five - 0.25 * q
    fp = split(factor)
    x5 = dot3(split(xs[...]), fp)
    square = split(dot3(fp, fp))
    fourth = dot3(square, square)
    xs[...] = 1.25 * x5 - 0.25 * dot3(split(fourth), split(dot3(split(q), split(x5))))

    root_copy = send(xs, xother, s_x, r_x, dev(dc=1))
    one_side = dot3(split(xs[...]), first_p)
    one_half = one_side.T[:, 128:]
    for k in (1, 2, 3):
        yk = wrap(y - k, NY)
        for q in block_copies(yk, c, s_6.at[k - 1], r_6.at[k - 1], dev(dy=k)):
            q.wait_recv()
        begin(block_copies(yk, c, s_7.at[k - 1], r_7.at[k - 1], dev(dc=1)))
    root_copy.wait_recv()
    other = xother[...]
    prec = dot3(
        split(jnp.where(c == 0, one_side, other)), split(jnp.where(c == 0, other[:, :128], one_half))
    ).reshape(32, 8, 128)
    p_square = jnp.sum(jnp.sum(prec * prec, axis=0), axis=0, keepdims=True)
    p_code = code_of(jnp.max(peak(prec), axis=0, keepdims=True))
    inverse = 1.0 / scale_of(p_code)
    end = jnp.concatenate([p_code] + sum_rows(g_square) + sum_rows(p_square) + [jnp.zeros((3, 128), F32)], axis=0)
    for i in range(NX * NZ):
        rows = (prec[i] * inverse + 12582912.0) - 12582912.0
        ma[i] = to16(jnp.concatenate([rows, end], axis=0))

    w = []
    for k in (4, 3, 5, 2, 6, 1, 7, 0):
        for j in (2, 1, 3, 0):
            if k or j:
                e = j * 8 + k
                w.append(send(ma.at[wrap(x + j, NX) * 8 + wrap(z + k, NZ)], rma.at[e], s_a.at[e], r_a.at[e], dev(dx=j, dz=k)))
    rma[0] = ma[grp]
    flush()
    put_stats(y, oc, DECAY * stats[y, oc] + dot3(second_p, first_p))

    def other_slot(k):
        yk = wrap(y - k, NY)
        for q in block_copies(yk, oc, s_7.at[k - 1], r_7.at[k - 1], dev(dc=1)):
            q.wait_recv()
        slot_stats(yk)

    def sums_of(end, at):
        return sums_from(end[at:at + 2]), sums_from(end[at + 2:at + 4])

    def add(pairs):
        while len(pairs) > 1:
            pairs = [(a[0] + b[0], a[1] + b[1]) for a, b in zip(pairs[::2], pairs[1::2])]
        return pairs[0]

    other_slot(1)
    for q in w:
        q.wait_recv()

    def pick(i, carry):
        pair = []
        for u in range(2):
            b = 2 * i + u
            o = owner[b]
            at = wrap(x - lax.div(o, NZ), NX) * 8 + wrap(z - lax.rem(o, NZ), NZ)
            pair.append(jnp.where(rank[b] == y, wide(rma[at]), jnp.zeros((16, 128), jnp.int32)))
            codes[pl.ds(lax.rem(b, 8), 1)] = pair[u][8:9].astype(F32)
        rows = jnp.concatenate([v[0:8] for v in pair], axis=0).astype(I16)
        my[lax.div(i, 4), pl.ds(pl.multiple_of(lax.rem(i, 4) * 16, 16), 16)] = rows
        return carry

    for yy in range(NY):
        lax.fori_loop(4 * yy, 4 * yy + 4, pick, 0)
        my[yy, pl.ds(64, 16)] = tail([codes[...]])
    w = []
    for k in (2, 1, 3):
        w.append(send(my.at[wrap(y + k, NY)], rmy.at[k], s_y.at[k], r_y.at[k], dev(dy=k)))
    g_sum, p_sum = add([sums_of(wide(rma[e]).astype(F32), 9) for e in range(NX * NZ)])
    flush()
    other_slot(2)
    for q in w:
        q.wait_recv()
    ends = [wide(v).astype(F32) for v in (my[y, pl.ds(64, 16)], rmy[1, pl.ds(64, 16)],
                                          rmy[2, pl.ds(64, 16)], rmy[3, pl.ds(64, 16)])]
    block_codes = (ends[0][0:8] + ends[1][0:8]) + (ends[2][0:8] + ends[3][0:8])
    fq[c, y, pl.ds(0, 64)] = (
        (wide(my[y, pl.ds(0, 64)]) + wide(rmy[1, pl.ds(0, 64)]))
        + (wide(rmy[2, pl.ds(0, 64)]) + wide(rmy[3, pl.ds(0, 64)]))
    ).astype(I16)
    fq[c, y, pl.ds(64, 16)] = tail([block_codes] + sum_rows(g_sum) + sum_rows(p_sum) + [jnp.zeros((4, 128), F32)])

    def ag_copy(core, yy, e, to):
        return remote(fq.at[core, yy], fq.at[core, yy], s_ag.at[e], r_ag.at[e], to)

    for k in (2, 1, 3, 0):
        for o in range(2):
            e = k * 2 + o
            if e:
                begin([ag_copy(c, y, e, dev(dy=k, dc=o))])
    other_slot(3)
    for k in range(NY):
        for o in range(2):
            e = k * 2 + o
            if e:
                ag_copy(wrap(c + o, 2), wrap(y - k, NY), e, dev(dy=k, dc=o)).wait_recv()
    g_sum, p_sum = add([sums_of(wide(fq[core, yy, pl.ds(64, 16)]).astype(F32), 8) for core in range(NC) for yy in range(NY)])
    ratio = jnp.sqrt(jnp.sum(g_sum, axis=1, keepdims=True) / jnp.sum(p_sum, axis=1, keepdims=True))
    ratio_ref[...] = jnp.broadcast_to(ratio, (1, 128))
    flush()


def hand_over(fq, ratio, ns_in, dir_out, ns_out, direction, sems):
    copies = []
    for i in range(SLOTS):
        for j in range(2):
            for half in range(2):
                at = (i, j, pl.ds(128 * half, 128))
                copies.append(pltpu.make_async_copy(ns_in.at[at], ns_out.at[at], sems.at[2 + len(copies)]))
    for q in copies:
        q.start()
    for half in range(2):
        for yy in (2 * half, 2 * half + 1):
            for h in range(NC):
                block_scales = scale_of(wide(fq[h, yy, pl.ds(64, 16)]).astype(F32)) * ratio[...]
                for i in range(8):
                    both = wide(fq[h, yy, pl.ds(16 * (i // 2), 16)]).astype(F32)
                    at = (yy * 8 + i) * 256 + h * 128
                    direction[:, pl.ds(at, 128)] = both[8 * (i % 2):8 * (i % 2) + 8] * block_scales[i:i + 1]
        at = (slice(None), pl.ds(4096 * half, 4096))
        copies.append(pltpu.make_async_copy(direction.at[at], dir_out.at[at], sems.at[half]))
        copies[-1].start()
    for q in copies:
        q.wait()


def local(grad_parts, stats, owner):
    grad = grad_parts.reshape(NY, NC, 32, 8192)
    vm, dma = pltpu.VMEM, pltpu.SemaphoreType.DMA
    t = (8, 128)
    scratch = [
        vm((SLOTS, 2, BS, BS), F32),
        vm((NY, 32, 8192), BF16), vm((NY, 32, 8192), BF16),
        vm((2, 2, 6, 272, 128), I16), vm((2, 2, 6, 272, 128), I16),
        vm((2, 2, 4, 4, 4) + t, F32),
        vm((2, 2, 4, 144, 128), I16), vm((2, 2, 4, 144, 128), I16),
        vm((2, 8, 4) + t, F32),
        vm((2, 8, 32, 128), I16), vm((2, 8, 32, 128), I16),
        vm((2, 8, 1, 128), F32), vm((2, 8, 1, 128), F32),
        vm((8, 32, 128), I16), vm((8, 32, 128), I16),
        vm((8, 1, 128), F32), vm((8, 1, 128), F32),
        vm((2, 16, 32, 128), I16), vm((2, 16, 32, 128), I16),
        vm((2, 16, 1, 128), F32), vm((2, 16, 1, 128), F32),
        vm((SLOTS, NC, 2, NY, 48, 128), I16),
        vm((NY, NC, 32, BS), F32),
        vm((8, 128), F32), vm((2, 4, 4) + t, F32),
        vm((BS, BS), F32), vm((BS, BS), F32), vm((BS, BS), F32),
        vm((32, 16, 128), I16), vm((32, 16, 128), I16),
        vm((NY, 80, 128), I16), vm((NY, 80, 128), I16),
        pltpu.SMEM((NB,), jnp.int32), pltpu.SMEM((NB,), jnp.int32), pltpu.SMEM((NX * SLOTS,), jnp.int32),
        dma, dma((10,)), dma, dma((10,)), dma((10,)), dma((2, 2, 6)), dma((2, 2, 6)),
        dma((2, 2, 4)), dma((2, 2, 4)), dma((2, 2, 8)), dma((2, 2, 8)), dma((2, 2, 7)), dma((2, 2, 7)),
        dma((2, 2, 16)), dma((2, 2, 16)),
        dma((2,)), dma((2,)), dma((3,)), dma((3,)), dma((3,)), dma((3,)), dma, dma,
        dma((32,)), dma((32,)), dma((4,)), dma((4,)), dma((8,)), dma((8,)),
    ]
    results = pl.pallas_call(
        kernel,
        out_shape=(pltpu.VMEM((NC, NY, 80, 128), I16), pltpu.VMEM((1, 128), F32), pltpu.VMEM((SLOTS, 2, BS, BS), F32)),
        in_specs=[
            pl.BlockSpec(memory_space=pltpu.HBM),
            pl.BlockSpec(memory_space=pltpu.HBM),
            pl.BlockSpec(memory_space=pltpu.HBM),
        ],
        out_specs=(pl.BlockSpec(memory_space=pltpu.VMEM),) * 3,
        scratch_shapes=scratch,
        compiler_params=pltpu.CompilerParams(
            collective_id=0, has_side_effects=True, vmem_limit_bytes=51 * 1024 * 1024
        ),
        cost_estimate=pl.CostEstimate(flops=4_000_000_000, bytes_accessed=9_000_000, transcendentals=0),
    )(*[pltpu.with_memory_space_constraint(v, pltpu.HBM) for v in (grad, stats, owner)])
    return pl.pallas_call(
        hand_over,
        out_shape=(
            jax.ShapeDtypeStruct((8, 8192), F32),
            jax.ShapeDtypeStruct((SLOTS, 2, BS, BS), F32),
        ),
        in_specs=[pl.BlockSpec(memory_space=pltpu.VMEM)] * 3,
        out_specs=(pl.BlockSpec(memory_space=pltpu.HBM), pl.BlockSpec(memory_space=pltpu.HBM)),
        scratch_shapes=[vm((8, 8192), F32), dma((2 + 4 * SLOTS,))],
    )(*[pltpu.with_memory_space_constraint(v, pltpu.VMEM) for v in results])


def solution(mesh):
    return jax.shard_map(
        local,
        mesh=mesh,
        in_specs=(P("rep", "grp", None, None), P("grp", None, None, None), P()),
        out_specs=(P("grp", None), P("grp", None, None, None)),
        check_vma=False,
    )
```

```python
import functools
import jax
import jax.numpy as jnp
from jax import lax
from jax.experimental import pallas as pl
from jax.experimental.pallas import tpu as pltpu
from jax.sharding import PartitionSpec as P

BS = 256
ITERS = 6
DECAY = 0.9
NX, NY, NZ, NC = 4, 4, 8, 2
NB, SLOTS = 32, 4
MESH = pl.DeviceIdType.MESH
F32, BF16, I16 = jnp.float32, jnp.bfloat16, jnp.int16
TOP = 32700.0


def split(a):
    hi = a.astype(BF16)
    return hi, (a - hi.astype(F32)).astype(BF16)


def dot3(a, b):
    rows = a[0].shape[0]
    both = jnp.dot(jnp.concatenate(a, axis=0), b[0], preferred_element_type=F32)
    return both[:rows] + (both[rows:] + jnp.dot(a[0], b[1], preferred_element_type=F32))


def scale_of(code):
    return jnp.exp2(code * 0.125) * (1.0 / TOP)


def code_of(top):
    return jnp.ceil(jnp.log2(jnp.maximum(top, 1e-30)) * 8.0)


def rounded(v, inverse):
    q = (v * inverse + 12582912.0) - 12582912.0
    return to16(q.reshape(v.shape[0] * 8, 128))


def peak(v):
    return jnp.max(jnp.abs(v), axis=0)


def narrow(v):
    code = code_of(jnp.max(peak(v), axis=0, keepdims=True))
    return rounded(v, 1.0 / scale_of(code)), code


def to16(v):
    return v.astype(jnp.int32).astype(I16)


def wide(q):
    return q.astype(jnp.int32)


def sum_rows(v):
    v = jnp.maximum(v, 1e-36)
    e = jnp.floor(jnp.log2(v))
    return [e, jnp.round((v * jnp.exp2(-e) - 1.0) * 16000.0)]


def sums_from(rows):
    return jnp.exp2(rows[0:1]) * (1.0 + rows[1:2] * (1.0 / 16000.0))


def tail(rows):
    left = 16 - sum(r.shape[0] for r in rows)
    zero = [jnp.zeros((left, 128), F32)] if left else []
    return to16(jnp.concatenate(list(rows) + zero, axis=0))


def kernel(
    grad, stats_hbm, owner_hbm,
    fq, ratio_ref, ns,
    stats, own, sib,
    m1, rm1, red, m2, rm2, s_buf, m3, rm3, c3, rc3, gx0, gx1, gc0, gc1, m5, rm5, c5, rc5, gq, gbuf, codes, acc,
    xs, qs, xother, ma, rma, my, rmy,
    owner, rank, local_j,
    s_owner, s_own, s_stat, s_sib, r_sib, s_1, r_1, s_2, r_2, s_3, r_3, s_4, r_4, s_5, r_5,
    s_d, r_d, s_6, r_6, s_7, r_7, s_x, r_x, s_a, r_a, s_y, r_y, s_ag, r_ag,
):
    gx, gc = (gx0, gx1), (gc0, gc1)
    rep, grp = lax.axis_index("rep"), lax.axis_index("grp")
    y, c = lax.div(rep, 2), lax.rem(rep, 2)
    x, z = lax.div(grp, 8), lax.rem(grp, 8)

    def wrap(v, n):
        return lax.rem(v + n, n)

    def dev(dy=0, dc=0, dx=0, dz=0):
        return (wrap(y + dy, NY) * 2 + wrap(c + dc, 2), wrap(x + dx, NX) * 8 + wrap(z + dz, NZ))

    pending = []

    def remote(src, dst, ssem, rsem, to):
        return pltpu.make_async_remote_copy(
            src_ref=src, dst_ref=dst, send_sem=ssem, recv_sem=rsem, device_id=to, device_id_type=MESH
        )

    def send(src, dst, ssem, rsem, to):
        copy = remote(src, dst, ssem, rsem, to)
        copy.start()
        pending.append(copy)
        return copy

    def flush():
        for q in pending:
            q.wait_send()
        pending.clear()

    def xcols(k):
        return pl.ds(pl.multiple_of(wrap(x + k, NX) * 1024, 1024), 1024)

    def chunk(axis, k, h, core=None):
        lead = () if core is None else (core,)
        if axis == 0:
            yy = pl.ds(0, 4) if h is None else pl.ds(2 * h, 2)
            return (yy,) + lead + (slice(None), xcols(k))
        cols = pl.ds(4096, 4096) if h is None else pl.ds(4096 + 2048 * h, 2048)
        return (wrap(y + k, NY),) + lead + (slice(None), cols)

    pieces_in_order = [(axis, k, h) for k, h in ((2, 0), (2, 1), (1, None), (-1, None), (0, None)) for axis in range(2)]
    def own_copy(i, axis, k, h):
        return pltpu.make_async_copy(grad.at[chunk(axis, k, h, c)], own.at[chunk(axis, k, h)], s_own.at[i])

    for i, piece in enumerate(pieces_in_order):
        own_copy(i, *piece).start()
    owner_copy = pltpu.make_async_copy(owner_hbm, owner, s_owner)
    owner_copy.start()
    stat_copy = pltpu.make_async_copy(stats_hbm, stats, s_stat)
    stat_copy.start()

    partners = [dict(dc=1)]
    partners += [dict(dx=j) for j in (1, -1, 2)] + [dict(dy=i) for i in (1, -1, 2)]
    partners += [dict(dz=k) for k in range(1, NZ)]
    barrier = pltpu.get_barrier_semaphore()
    for p in partners:
        pl.semaphore_signal(barrier, inc=1, device_id=dev(**p), device_id_type=MESH)
    pl.semaphore_wait(barrier, len(partners))

    oc = wrap(c + 1, 2)
    def sib_copy(i, axis, k, h):
        return remote(grad.at[chunk(axis, k, h, oc)], sib.at[chunk(axis, k, h)], s_sib.at[i], r_sib.at[i], dev(dc=1))

    def begin(copies):
        for q in copies:
            q.start()
            pending.append(q)

    for i, piece in enumerate(pieces_in_order):
        begin([sib_copy(i, *piece)])

    def ready(i, axis, k, h):
        own_copy(i, axis, k, h).wait()
        sib_copy(i, axis, k, h).wait_recv()

    def tile(v):
        return v.reshape(4, 8, 128)

    def unit(axis, k, h, a, b):
        if axis == 0:
            row, at = 2 * h + a, wrap(x + k, NX) * 1024 + b * 128
        else:
            row, at = wrap(y + k, NY), 4096 + 2048 * h + (a * 8 + b) * 128
        at = pl.ds(pl.multiple_of(at, 128), 128)
        return own[row, :, at].astype(F32) + sib[row, :, at].astype(F32)

    def unit_rows(n):
        return pl.ds(n * 32 if isinstance(n, int) else pl.multiple_of(n * 32, 32), 32)

    def scale_tile(rows):
        return scale_of(wide(rows).astype(F32)[0:8])

    def scale_tile(rows):
        return scale_of(wide(rows).astype(F32)[0:8])

    def part(u, axis, k, h, adds, flow):
        scales = [scale_tile(rm1[u, axis, f, pl.ds(256, 16)]) for f in adds]
        zero = jnp.zeros((8, 128), F32)
        tops = [zero, zero]
        for a in range(2):
            for i in range(4):
                v = tile(unit(axis, k, h, a, 2 * i + u))
                for f, scale in zip(adds, scales):
                    v = v + tile(wide(rm1[u, axis, f, unit_rows(4 * a + i)]).astype(F32)) * scale
                if flow is None:
                    red[u, axis, 2 * h + a, i] = v
                else:
                    acc[a, i] = v
                tops[a] = jnp.maximum(tops[a], peak(v))
        if flow is not None:
            tops = [jnp.maximum(tops[0], tops[1])] * 2
        codes = [code_of(t) for t in tops]
        inverse = [1.0 / scale_of(code) for code in codes]
        for a in range(2):
            for i in range(4):
                if flow is None:
                    m2[u, axis, 2 * h + a, unit_rows(i)] = rounded(red[u, axis, 2 * h + a, i], inverse[a])
                else:
                    m1[u, axis, flow, unit_rows(4 * a + i)] = rounded(acc[a, i], inverse[a])
            if flow is None:
                m2[u, axis, 2 * h + a, pl.ds(128, 16)] = tail([codes[a]])
        if flow is not None:
            m1[u, axis, flow, pl.ds(256, 16)] = tail([codes[0]])

    def flow_copy(u, axis, f, hop):
        to = dev(dx=hop) if axis == 0 else dev(dy=hop)
        return remote(m1.at[u, axis, f], rm1.at[u, axis, f], s_1.at[u, axis, f], r_1.at[u, axis, f], to)

    def arrived(u, axis, f):
        flow_copy(u, axis, f, 1).wait_recv()

    def far(u):
        def body(h, carry):
            for axis in range(2):
                if u == 0:
                    ready(2 * h + axis, axis, 2, h)
                part(u, axis, 2, h, [], h)
                flow_copy(u, axis, h, 1 - 2 * h).start()
            return carry

        lax.fori_loop(0, 2, body, 0)

    def near(u):
        def body(h, carry):
            hop = 2 * h - 1
            for axis in range(2):
                if u == 0:
                    ready(6 - 2 * h + axis, axis, hop, None)
                part(u, axis, hop, h, [], 2 + h)
                flow_copy(u, axis, 2 + h, hop).start()
            return carry

        lax.fori_loop(0, 2, body, 0)

    def onward(u):
        def body(h, carry):
            hop = 1 - 2 * h
            for axis in range(2):
                arrived(u, axis, h)
                part(u, axis, hop, h, [h], 4 + h)
                flow_copy(u, axis, 4 + h, hop).start()
            return carry

        lax.fori_loop(0, 2, body, 0)
        for axis in range(2):
            for f in range(6):
                pending.append(flow_copy(u, axis, f, 1))

    def p2_copy(u, axis, to, at, frm):
        return remote(m2.at[u, axis, to], rm2.at[u, axis, frm], s_2.at[u, axis, to], r_2.at[u, axis, frm], at)

    def p2_send(u, axis, to):
        me = (y, x)[axis]
        at = dev(dy=to - y) if axis == 0 else dev(dx=to - x)

        @pl.when(me != to)
        def _():
            p2_copy(u, axis, to, at, me).start()

    def last(u):
        def body(h, carry):
            for axis in range(2):
                arrived(u, axis, 2 + h)
                arrived(u, axis, 4 + h)
                part(u, axis, 0, h, [2 + h, 4 + h], None)
                p2_send(u, axis, 2 * h)
                p2_send(u, axis, 2 * h + 1)
            return carry

        if u == 0:
            for axis in range(2):
                ready(8 + axis, axis, 0, None)
        lax.fori_loop(0, 2, body, 0)

    def p3_copies(u, to, at, frm):
        return (remote(c3.at[u, to], rc3.at[u, frm], s_3.at[u, 0, to], r_3.at[u, 0, frm], at),
                remote(m3.at[u, to], rm3.at[u, frm], s_3.at[u, 1, to], r_3.at[u, 1, frm], at))

    def column_code(v):
        return code_of(jnp.max(peak(v), axis=0, keepdims=True))

    def along_z(u):
        scales = {}
        for axis in range(2):
            me = (y, x)[axis]
            for k in range(1, 4):
                frm = wrap(me - k, 4)
                q = p2_copy(u, axis, wrap(me + k, 4), dev(dc=1), frm)
                pending.append(q)
                q.wait_recv()
                scales[axis, k] = scale_tile(rm2[u, axis, frm, pl.ds(128, 16)])

        def sum2(j, carry):
            for axis in range(2):
                me = (y, x)[axis]
                v = red[u, axis, me, j]
                for k in range(1, 4):
                    v = v + tile(wide(rm2[u, axis, wrap(me - k, 4), unit_rows(j)]).astype(F32)) * scales[axis, k]
                to = 4 * axis + j
                s_buf[u, to] = v
                code = column_code(v)
                c3[u, to] = code
                m3[u, to] = rounded(v, 1.0 / scale_of(code))

                @pl.when(z != to)
                def _():
                    for q in p3_copies(u, to, dev(dz=to - z), z):
                        q.start()

            return carry

        lax.fori_loop(0, 4, sum2, 0)

    def p4_copies(u, src, k):
        return (remote(gc[u].at[src], gc[u].at[src], s_4.at[u, 0, k - 1], r_4.at[u, 0, k - 1], dev(dz=k)),
                remote(gx[u].at[src], gx[u].at[src], s_4.at[u, 1, k - 1], r_4.at[u, 1, k - 1], dev(dz=k)))

    def gather_z(u):
        piece = s_buf[u, z]
        for k in range(1, NZ):
            for q in p3_copies(u, wrap(z + k, NZ), dev(dc=1), wrap(z - k, NZ)):
                pending.append(q)
                q.wait_recv()
        for k in range(1, NZ):
            frm = wrap(z - k, NZ)
            piece = piece + tile(wide(rm3[u, frm]).astype(F32)) * scale_of(rc3[u, frm])
        piece = piece * (1.0 / 256.0)
        code = column_code(piece)
        gc[u][z] = code
        gx[u][z] = rounded(piece, 1.0 / scale_of(code))
        for k in (4, 3, 5, 2, 6, 1, 7):
            begin(p4_copies(u, z, k))
        return piece

    def p5_copies(u, e):
        at = dev(dy=e // 4, dx=e % 4)
        return (remote(c5.at[u, e], rc5.at[u, e], s_5.at[u, 0, e], r_5.at[u, 0, e], at),
                remote(m5.at[u, e], rm5.at[u, e], s_5.at[u, 1, e], r_5.at[u, 1, e], at))

    def route(u):
        for k in range(1, NZ):
            for q in p4_copies(u, wrap(z - k, NZ), k):
                q.wait_recv()
        for i in (2, 1, 3, 0):
            for j in (2, 1, 3, 0):
                e = i * 4 + j
                which = local_j[wrap(x + j, NX) * SLOTS + wrap(y + i, NY)]
                take = jnp.maximum(which, 0)
                c5[u, e] = jnp.where(which >= 0, gc[u][take], jnp.zeros((1, 128), F32))
                m5[u, e] = jnp.where(which >= 0, wide(gx[u][take]), jnp.zeros((32, 128), jnp.int32)).astype(I16)
                if e:
                    begin(p5_copies(u, e))

    def half_copy(u, core):
        return remote(gq.at[y, core, u], gq.at[y, core, u], s_d.at[u], r_d.at[u], dev(dc=1))

    def open_half(slot, core, u):
        for i in range(NY):
            scale = scale_of(wide(gq[slot, core, u, i, pl.ds(32, 16)]).astype(F32)[0:1])
            v = tile(wide(gq[slot, core, u, i, pl.ds(0, 32)]).astype(F32)) * scale
            gbuf[i, core, :, pl.ds(u * 128, 128)] = v.reshape(32, 128)

    def collect(u):
        for i in range(NY):
            parts = [(m5[u, 0], c5[u, 0])] if i == 0 else []
            for j in range(NX):
                e = i * 4 + j
                if e:
                    for q in p5_copies(u, e):
                        q.wait_recv()
                    parts.append((rm5[u, e], rc5[u, e]))
            rows = [wide(v[0]) for v in parts]
            yi = wrap(y - i, NY)
            gq[y, c, u, yi, pl.ds(0, 32)] = ((rows[0] + rows[1]) + (rows[2] + rows[3])).astype(I16)
            code = (parts[0][1] + parts[1][1]) + (parts[2][1] + parts[3][1])
            gq[y, c, u, yi, pl.ds(32, 16)] = tail([code])
        begin([half_copy(u, c)])

    def rank_row(b, carry):
        ob = owner[b]
        total = jnp.int32(0)
        for e in range(NB):
            total = total + jnp.where((owner[e] == ob) & (e < b), 1, 0)
        rank[b] = total
        return carry

    def find(i, carry):
        target = lax.div(i, SLOTS) * NZ + z
        slot = lax.rem(i, SLOTS)
        found = jnp.int32(-1)
        for j in range(8):
            b = 4 * x + j if j < 4 else 16 + 4 * x + j - 4
            found = jnp.where((owner[b] == target) & (rank[b] == slot), j, found)
        local_j[i] = found
        return carry

    far(0)
    near(0)
    far(1)
    onward(0)
    near(1)
    onward(1)
    owner_copy.wait()
    lax.fori_loop(0, NB, rank_row, 0)
    last(0)
    last(1)
    along_z(0)
    along_z(1)
    lax.fori_loop(0, NX * SLOTS, find, 0)
    n_mine = jnp.int32(0)
    for b in range(NB):
        n_mine = n_mine + jnp.where(owner[b] == grp, 1, 0)
    pieces = [gather_z(u) for u in range(2)]
    route(0)
    route(1)
    collect(0)
    collect(1)
    g_square = jnp.sum(jnp.sum(pieces[0] * pieces[0] + pieces[1] * pieces[1], axis=0), axis=0, keepdims=True)

    def block_copies(slot, core, ssem, rsem, to):
        return [remote(gq.at[slot, core], gq.at[slot, core], ssem, rsem, to)]

    for k in (2, 1, 3):
        begin(block_copies(y, c, s_6.at[k - 1], r_6.at[k - 1], dev(dy=k)))
    stat_copy.wait()
    for u in range(2):
        open_half(y, c, u)
    for u in range(2):
        half_copy(u, oc).wait_recv()
        open_half(y, oc, u)

    def put_stats(slot, side, value):
        ns[slot, side] = jnp.where(n_mine > slot, value, stats[slot, side])

    def slot_stats(slot):
        for core in range(NC):
            for u in range(2):
                open_half(slot, core, u)
        g = gbuf[...].reshape(BS, BS)
        gp, gtp = split(g), split(g.T)
        put_stats(slot, 0, DECAY * stats[slot, 0] + dot3(gp, gtp))
        put_stats(slot, 1, DECAY * stats[slot, 1] + dot3(gtp, gp))

    g = gbuf[...].reshape(BS, BS)
    gt = g.T
    first, second = jnp.where(c == 0, g, gt), jnp.where(c == 0, gt, g)
    first_p, second_p = split(first), split(second)
    mat = DECAY * stats[y, c] + dot3(first_p, second_p)
    put_stats(y, c, mat)
    norm = jnp.sqrt(jnp.sum(jnp.sum(mat * mat, axis=0, keepdims=True), axis=1, keepdims=True))
    five = jnp.where(
        lax.broadcasted_iota(jnp.int32, (BS, BS), 0) == lax.broadcasted_iota(jnp.int32, (BS, BS), 1), 1.25, 0.0
    ).astype(F32)
    q0 = mat * (1.0 / norm)
    factor = five - 0.25 * q0
    xs[...] = factor * lax.rsqrt(jnp.sqrt(norm))

    def newton(i, carry):
        q = qs[...]
        fp = split(five - 0.25 * q)
        square = split(dot3(fp, fp))
        x_next = dot3(split(xs[...]), fp)
        qs[...] = dot3(split(dot3(square, square)), split(q))
        xs[...] = x_next
        return carry

    fp = split(factor)
    square = split(dot3(fp, fp))
    qs[...] = dot3(split(dot3(square, square)), split(q0))
    lax.fori_loop(0, ITERS - 3, newton, 0)
    q = qs[...]
    factor = five - 0.25 * q
    fp = split(factor)
    x5 = dot3(split(xs[...]), fp)
    square = split(dot3(fp, fp))
    fourth = dot3(square, square)
    xs[...] = 1.25 * x5 - 0.25 * dot3(split(fourth), split(dot3(split(q), split(x5))))

    root_copy = send(xs, xother, s_x, r_x, dev(dc=1))
    one_side = dot3(split(xs[...]), first_p)
    one_half = one_side.T[:, 128:]
    for k in (1, 2, 3):
        yk = wrap(y - k, NY)
        for q in block_copies(yk, c, s_6.at[k - 1], r_6.at[k - 1], dev(dy=k)):
            q.wait_recv()
        begin(block_copies(yk, c, s_7.at[k - 1], r_7.at[k - 1], dev(dc=1)))
    root_copy.wait_recv()
    other = xother[...]
    prec = dot3(
        split(jnp.where(c == 0, one_side, other)), split(jnp.where(c == 0, other[:, :128], one_half))
    ).reshape(32, 8, 128)
    p_square = jnp.sum(jnp.sum(prec * prec, axis=0), axis=0, keepdims=True)
    p_code = code_of(jnp.max(peak(prec), axis=0, keepdims=True))
    inverse = 1.0 / scale_of(p_code)
    end = jnp.concatenate([p_code] + sum_rows(g_square) + sum_rows(p_square) + [jnp.zeros((3, 128), F32)], axis=0)
    for i in range(NX * NZ):
        rows = (prec[i] * inverse + 12582912.0) - 12582912.0
        ma[i] = to16(jnp.concatenate([rows, end], axis=0))

    w = []
    for k in (4, 3, 5, 2, 6, 1, 7, 0):
        for j in (2, 1, 3, 0):
            if k or j:
                e = j * 8 + k
                w.append(send(ma.at[wrap(x + j, NX) * 8 + wrap(z + k, NZ)], rma.at[e], s_a.at[e], r_a.at[e], dev(dx=j, dz=k)))
    rma[0] = ma[grp]
    flush()
    put_stats(y, oc, DECAY * stats[y, oc] + dot3(second_p, first_p))

    def other_slot(k):
        yk = wrap(y - k, NY)
        for q in block_copies(yk, oc, s_7.at[k - 1], r_7.at[k - 1], dev(dc=1)):
            q.wait_recv()
        slot_stats(yk)

    def sums_of(end, at):
        return sums_from(end[at:at + 2]), sums_from(end[at + 2:at + 4])

    def add(pairs):
        while len(pairs) > 1:
            pairs = [(a[0] + b[0], a[1] + b[1]) for a, b in zip(pairs[::2], pairs[1::2])]
        return pairs[0]

    other_slot(1)
    for q in w:
        q.wait_recv()

    def pick(i, carry):
        pair = []
        for u in range(2):
            b = 2 * i + u
            o = owner[b]
            at = wrap(x - lax.div(o, NZ), NX) * 8 + wrap(z - lax.rem(o, NZ), NZ)
            pair.append(jnp.where(rank[b] == y, wide(rma[at]), jnp.zeros((16, 128), jnp.int32)))
            codes[pl.ds(lax.rem(b, 8), 1)] = pair[u][8:9].astype(F32)
        rows = jnp.concatenate([v[0:8] for v in pair], axis=0).astype(I16)
        my[lax.div(i, 4), pl.ds(pl.multiple_of(lax.rem(i, 4) * 16, 16), 16)] = rows
        return carry

    w = []
    for k in (2, 1, 3, 0):
        yy = wrap(y + k, NY)
        lax.fori_loop(4 * yy, 4 * yy + 4, pick, 0)
        my[yy, pl.ds(64, 16)] = tail([codes[...]])
        if k:
            w.append(send(my.at[yy], rmy.at[k], s_y.at[k], r_y.at[k], dev(dy=k)))
    g_sum, p_sum = add([sums_of(wide(rma[e]).astype(F32), 9) for e in range(NX * NZ)])
    flush()
    other_slot(2)
    for q in w:
        q.wait_recv()
    ends = [wide(v).astype(F32) for v in (my[y, pl.ds(64, 16)], rmy[1, pl.ds(64, 16)],
                                          rmy[2, pl.ds(64, 16)], rmy[3, pl.ds(64, 16)])]
    block_codes = (ends[0][0:8] + ends[1][0:8]) + (ends[2][0:8] + ends[3][0:8])
    fq[c, y, pl.ds(0, 64)] = (
        (wide(my[y, pl.ds(0, 64)]) + wide(rmy[1, pl.ds(0, 64)]))
        + (wide(rmy[2, pl.ds(0, 64)]) + wide(rmy[3, pl.ds(0, 64)]))
    ).astype(I16)
    fq[c, y, pl.ds(64, 16)] = tail([block_codes] + sum_rows(g_sum) + sum_rows(p_sum) + [jnp.zeros((4, 128), F32)])

    def ag_copy(core, yy, e, to):
        return remote(fq.at[core, yy], fq.at[core, yy], s_ag.at[e], r_ag.at[e], to)

    for k in (2, 1, 3, 0):
        for o in range(2):
            e = k * 2 + o
            if e:
                begin([ag_copy(c, y, e, dev(dy=k, dc=o))])
    other_slot(3)
    for k in range(NY):
        for o in range(2):
            e = k * 2 + o
            if e:
                ag_copy(wrap(c + o, 2), wrap(y - k, NY), e, dev(dy=k, dc=o)).wait_recv()
    g_sum, p_sum = add([sums_of(wide(fq[core, yy, pl.ds(64, 16)]).astype(F32), 8) for core in range(NC) for yy in range(NY)])
    ratio = jnp.sqrt(jnp.sum(g_sum, axis=1, keepdims=True) / jnp.sum(p_sum, axis=1, keepdims=True))
    ratio_ref[...] = jnp.broadcast_to(ratio, (1, 128))
    flush()


def hand_over(fq, ratio, ns_in, dir_out, ns_out, direction, sems):
    copies = []
    for i in range(SLOTS):
        for j in range(2):
            for half in range(2):
                at = (i, j, pl.ds(128 * half, 128))
                copies.append(pltpu.make_async_copy(ns_in.at[at], ns_out.at[at], sems.at[2 + len(copies)]))
    for q in copies:
        q.start()
    for half in range(2):
        for yy in (2 * half, 2 * half + 1):
            for h in range(NC):
                block_scales = scale_of(wide(fq[h, yy, pl.ds(64, 16)]).astype(F32)) * ratio[...]
                for i in range(8):
                    both = wide(fq[h, yy, pl.ds(16 * (i // 2), 16)]).astype(F32)
                    at = (yy * 8 + i) * 256 + h * 128
                    direction[:, pl.ds(at, 128)] = both[8 * (i % 2):8 * (i % 2) + 8] * block_scales[i:i + 1]
        at = (slice(None), pl.ds(4096 * half, 4096))
        copies.append(pltpu.make_async_copy(direction.at[at], dir_out.at[at], sems.at[half]))
        copies[-1].start()
    for q in copies:
        q.wait()


def local(grad_parts, stats, owner):
    grad = grad_parts.reshape(NY, NC, 32, 8192)
    vm, dma = pltpu.VMEM, pltpu.SemaphoreType.DMA
    t = (8, 128)
    scratch = [
        vm((SLOTS, 2, BS, BS), F32),
        vm((NY, 32, 8192), BF16), vm((NY, 32, 8192), BF16),
        vm((2, 2, 6, 272, 128), I16), vm((2, 2, 6, 272, 128), I16),
        vm((2, 2, 4, 4, 4) + t, F32),
        vm((2, 2, 4, 144, 128), I16), vm((2, 2, 4, 144, 128), I16),
        vm((2, 8, 4) + t, F32),
        vm((2, 8, 32, 128), I16), vm((2, 8, 32, 128), I16),
        vm((2, 8, 1, 128), F32), vm((2, 8, 1, 128), F32),
        vm((8, 32, 128), I16), vm((8, 32, 128), I16),
        vm((8, 1, 128), F32), vm((8, 1, 128), F32),
        vm((2, 16, 32, 128), I16), vm((2, 16, 32, 128), I16),
        vm((2, 16, 1, 128), F32), vm((2, 16, 1, 128), F32),
        vm((SLOTS, NC, 2, NY, 48, 128), I16),
        vm((NY, NC, 32, BS), F32),
        vm((8, 128), F32), vm((2, 4, 4) + t, F32),
        vm((BS, BS), F32), vm((BS, BS), F32), vm((BS, BS), F32),
        vm((32, 16, 128), I16), vm((32, 16, 128), I16),
        vm((NY, 80, 128), I16), vm((NY, 80, 128), I16),
        pltpu.SMEM((NB,), jnp.int32), pltpu.SMEM((NB,), jnp.int32), pltpu.SMEM((NX * SLOTS,), jnp.int32),
        dma, dma((10,)), dma, dma((10,)), dma((10,)), dma((2, 2, 6)), dma((2, 2, 6)),
        dma((2, 2, 4)), dma((2, 2, 4)), dma((2, 2, 8)), dma((2, 2, 8)), dma((2, 2, 7)), dma((2, 2, 7)),
        dma((2, 2, 16)), dma((2, 2, 16)),
        dma((2,)), dma((2,)), dma((3,)), dma((3,)), dma((3,)), dma((3,)), dma, dma,
        dma((32,)), dma((32,)), dma((4,)), dma((4,)), dma((8,)), dma((8,)),
    ]
    results = pl.pallas_call(
        kernel,
        out_shape=(pltpu.VMEM((NC, NY, 80, 128), I16), pltpu.VMEM((1, 128), F32), pltpu.VMEM((SLOTS, 2, BS, BS), F32)),
        in_specs=[
            pl.BlockSpec(memory_space=pltpu.HBM),
            pl.BlockSpec(memory_space=pltpu.HBM),
            pl.BlockSpec(memory_space=pltpu.HBM),
        ],
        out_specs=(pl.BlockSpec(memory_space=pltpu.VMEM),) * 3,
        scratch_shapes=scratch,
        compiler_params=pltpu.CompilerParams(
            collective_id=0, has_side_effects=True, vmem_limit_bytes=51 * 1024 * 1024
        ),
        cost_estimate=pl.CostEstimate(flops=4_000_000_000, bytes_accessed=9_000_000, transcendentals=0),
    )(*[pltpu.with_memory_space_constraint(v, pltpu.HBM) for v in (grad, stats, owner)])
    return pl.pallas_call(
        hand_over,
        out_shape=(
            jax.ShapeDtypeStruct((8, 8192), F32),
            jax.ShapeDtypeStruct((SLOTS, 2, BS, BS), F32),
        ),
        in_specs=[pl.BlockSpec(memory_space=pltpu.VMEM)] * 3,
        out_specs=(pl.BlockSpec(memory_space=pltpu.HBM), pl.BlockSpec(memory_space=pltpu.HBM)),
        scratch_shapes=[vm((8, 8192), F32), dma((2 + 4 * SLOTS,))],
    )(*[pltpu.with_memory_space_constraint(v, pltpu.VMEM) for v in results])


def solution(mesh):
    return jax.shard_map(
        local,
        mesh=mesh,
        in_specs=(P("rep", "grp", None, None), P("grp", None, None, None), P()),
        out_specs=(P("grp", None), P("grp", None, None, None)),
        check_vma=False,
    )
```

```python
import functools
import jax
import jax.numpy as jnp
from jax import lax
from jax.experimental import pallas as pl
from jax.experimental.pallas import tpu as pltpu
from jax.sharding import PartitionSpec as P

BS = 256
ITERS = 6
DECAY = 0.9
NX, NY, NZ, NC = 4, 4, 8, 2
NB, SLOTS = 32, 4
MESH = pl.DeviceIdType.MESH
F32, BF16, I16 = jnp.float32, jnp.bfloat16, jnp.int16
TOP = 32700.0


def split(a):
    hi = a.astype(BF16)
    return hi, (a - hi.astype(F32)).astype(BF16)


def dot3(a, b):
    rows = a[0].shape[0]
    both = jnp.dot(jnp.concatenate(a, axis=0), b[0], preferred_element_type=F32)
    return both[:rows] + (both[rows:] + jnp.dot(a[0], b[1], preferred_element_type=F32))


def scale_of(code):
    return jnp.exp2(code * 0.125) * (1.0 / TOP)


def code_of(top):
    return jnp.ceil(jnp.log2(jnp.maximum(top, 1e-30)) * 8.0)


def rounded(v, inverse):
    q = (v * inverse + 12582912.0) - 12582912.0
    return to16(q.reshape(v.shape[0] * 8, 128))


def peak(v):
    return jnp.max(jnp.abs(v), axis=0)


def narrow(v):
    code = code_of(jnp.max(peak(v), axis=0, keepdims=True))
    return rounded(v, 1.0 / scale_of(code)), code


def to16(v):
    return v.astype(jnp.int32).astype(I16)


def wide(q):
    return q.astype(jnp.int32)


def sum_rows(v):
    v = jnp.maximum(v, 1e-36)
    e = jnp.floor(jnp.log2(v))
    return [e, jnp.round((v * jnp.exp2(-e) - 1.0) * 16000.0)]


def sums_from(rows):
    return jnp.exp2(rows[0:1]) * (1.0 + rows[1:2] * (1.0 / 16000.0))


def tail(rows):
    left = 16 - sum(r.shape[0] for r in rows)
    zero = [jnp.zeros((left, 128), F32)] if left else []
    return to16(jnp.concatenate(list(rows) + zero, axis=0))


def kernel(
    grad, stats_hbm, owner_hbm,
    fq, ratio_ref, ns,
    stats, own, sib,
    m1, rm1, red, m2, rm2, s_buf, m3, rm3, c3, rc3, gx0, gx1, gc0, gc1, m5, rm5, c5, rc5, gq, gbuf, codes, acc,
    xs, qs, xother, pbuf, ma, rma, my, rmy,
    owner, rank, local_j,
    s_owner, s_own, s_stat, s_sib, r_sib, s_1, r_1, s_2, r_2, s_3, r_3, s_4, r_4, s_5, r_5,
    s_d, r_d, s_6, r_6, s_7, r_7, s_x, r_x, s_a, r_a, s_y, r_y, s_ag, r_ag,
):
    gx, gc = (gx0, gx1), (gc0, gc1)
    rep, grp = lax.axis_index("rep"), lax.axis_index("grp")
    y, c = lax.div(rep, 2), lax.rem(rep, 2)
    x, z = lax.div(grp, 8), lax.rem(grp, 8)

    def wrap(v, n):
        return lax.rem(v + n, n)

    def dev(dy=0, dc=0, dx=0, dz=0):
        return (wrap(y + dy, NY) * 2 + wrap(c + dc, 2), wrap(x + dx, NX) * 8 + wrap(z + dz, NZ))

    pending = []

    def remote(src, dst, ssem, rsem, to):
        return pltpu.make_async_remote_copy(
            src_ref=src, dst_ref=dst, send_sem=ssem, recv_sem=rsem, device_id=to, device_id_type=MESH
        )

    def send(src, dst, ssem, rsem, to):
        copy = remote(src, dst, ssem, rsem, to)
        copy.start()
        pending.append(copy)
        return copy

    def flush():
        for q in pending:
            q.wait_send()
        pending.clear()

    def xcols(k):
        return pl.ds(pl.multiple_of(wrap(x + k, NX) * 1024, 1024), 1024)

    def chunk(axis, k, h, core=None):
        lead = () if core is None else (core,)
        if axis == 0:
            yy = pl.ds(0, 4) if h is None else pl.ds(2 * h, 2)
            return (yy,) + lead + (slice(None), xcols(k))
        cols = pl.ds(4096, 4096) if h is None else pl.ds(4096 + 2048 * h, 2048)
        return (wrap(y + k, NY),) + lead + (slice(None), cols)

    pieces_in_order = [(axis, k, h) for k, h in ((2, 0), (2, 1), (1, None), (-1, None), (0, None)) for axis in range(2)]
    def own_copy(i, axis, k, h):
        return pltpu.make_async_copy(grad.at[chunk(axis, k, h, c)], own.at[chunk(axis, k, h)], s_own.at[i])

    partners = [dict(dc=1)]
    partners += [dict(dx=j) for j in (1, -1, 2)] + [dict(dy=i) for i in (1, -1, 2)]
    partners += [dict(dz=k) for k in range(1, NZ)]
    barrier = pltpu.get_barrier_semaphore()
    for p in partners:
        pl.semaphore_signal(barrier, inc=1, device_id=dev(**p), device_id_type=MESH)
    for i, piece in enumerate(pieces_in_order):
        own_copy(i, *piece).start()
    owner_copy = pltpu.make_async_copy(owner_hbm, owner, s_owner)
    owner_copy.start()
    stat_copy = pltpu.make_async_copy(stats_hbm, stats, s_stat)
    stat_copy.start()

    pl.semaphore_wait(barrier, len(partners))

    oc = wrap(c + 1, 2)
    def sib_copy(i, axis, k, h):
        return remote(grad.at[chunk(axis, k, h, oc)], sib.at[chunk(axis, k, h)], s_sib.at[i], r_sib.at[i], dev(dc=1))

    def begin(copies):
        for q in copies:
            q.start()
            pending.append(q)

    for i, piece in enumerate(pieces_in_order):
        begin([sib_copy(i, *piece)])

    def ready(i, axis, k, h):
        own_copy(i, axis, k, h).wait()
        sib_copy(i, axis, k, h).wait_recv()

    def tile(v):
        return v.reshape(4, 8, 128)

    def unit(axis, k, h, a, b):
        if axis == 0:
            row, at = 2 * h + a, wrap(x + k, NX) * 1024 + b * 128
        else:
            row, at = wrap(y + k, NY), 4096 + 2048 * h + (a * 8 + b) * 128
        at = pl.ds(pl.multiple_of(at, 128), 128)
        return own[row, :, at].astype(F32) + sib[row, :, at].astype(F32)

    def unit_rows(n):
        return pl.ds(n * 32 if isinstance(n, int) else pl.multiple_of(n * 32, 32), 32)

    def scale_tile(rows):
        return scale_of(wide(rows).astype(F32)[0:8])

    def scale_tile(rows):
        return scale_of(wide(rows).astype(F32)[0:8])

    def part(u, axis, k, h, adds, flow):
        scales = [scale_tile(rm1[u, axis, f, pl.ds(256, 16)]) for f in adds]
        zero = jnp.zeros((8, 128), F32)
        tops = [zero, zero]
        for a in range(2):
            for i in range(4):
                v = tile(unit(axis, k, h, a, 2 * i + u))
                for f, scale in zip(adds, scales):
                    v = v + tile(wide(rm1[u, axis, f, unit_rows(4 * a + i)]).astype(F32)) * scale
                if flow is None:
                    red[u, axis, 2 * h + a, i] = v
                else:
                    acc[a, i] = v
                tops[a] = jnp.maximum(tops[a], peak(v))
        if flow is not None:
            tops = [jnp.maximum(tops[0], tops[1])] * 2
        codes = [code_of(t) for t in tops]
        inverse = [1.0 / scale_of(code) for code in codes]
        for a in range(2):
            for i in range(4):
                if flow is None:
                    m2[u, axis, 2 * h + a, unit_rows(i)] = rounded(red[u, axis, 2 * h + a, i], inverse[a])
                else:
                    m1[u, axis, flow, unit_rows(4 * a + i)] = rounded(acc[a, i], inverse[a])
            if flow is None:
                m2[u, axis, 2 * h + a, pl.ds(128, 16)] = tail([codes[a]])
        if flow is not None:
            m1[u, axis, flow, pl.ds(256, 16)] = tail([codes[0]])

    def flow_copy(u, axis, f, hop):
        to = dev(dx=hop) if axis == 0 else dev(dy=hop)
        return remote(m1.at[u, axis, f], rm1.at[u, axis, f], s_1.at[u, axis, f], r_1.at[u, axis, f], to)

    def arrived(u, axis, f):
        flow_copy(u, axis, f, 1).wait_recv()

    def far(u):
        def body(h, carry):
            for axis in range(2):
                if u == 0:
                    ready(2 * h + axis, axis, 2, h)
                part(u, axis, 2, h, [], h)
                flow_copy(u, axis, h, 1 - 2 * h).start()
            return carry

        lax.fori_loop(0, 2, body, 0)

    def near(u):
        def body(h, carry):
            hop = 2 * h - 1
            for axis in range(2):
                if u == 0:
                    ready(6 - 2 * h + axis, axis, hop, None)
                part(u, axis, hop, h, [], 2 + h)
                flow_copy(u, axis, 2 + h, hop).start()
            return carry

        lax.fori_loop(0, 2, body, 0)

    def onward(u):
        def body(h, carry):
            hop = 1 - 2 * h
            for axis in range(2):
                arrived(u, axis, h)
                part(u, axis, hop, h, [h], 4 + h)
                flow_copy(u, axis, 4 + h, hop).start()
            return carry

        lax.fori_loop(0, 2, body, 0)
        for axis in range(2):
            for f in range(6):
                pending.append(flow_copy(u, axis, f, 1))

    def p2_copy(u, axis, to, at, frm):
        return remote(m2.at[u, axis, to], rm2.at[u, axis, frm], s_2.at[u, axis, to], r_2.at[u, axis, frm], at)

    def p2_send(u, axis, to):
        me = (y, x)[axis]
        at = dev(dy=to - y) if axis == 0 else dev(dx=to - x)

        @pl.when(me != to)
        def _():
            p2_copy(u, axis, to, at, me).start()

    def last(u):
        def body(h, carry):
            for axis in range(2):
                arrived(u, axis, 2 + h)
                arrived(u, axis, 4 + h)
                part(u, axis, 0, h, [2 + h, 4 + h], None)
                p2_send(u, axis, 2 * h)
                p2_send(u, axis, 2 * h + 1)
            return carry

        if u == 0:
            for axis in range(2):
                ready(8 + axis, axis, 0, None)
        lax.fori_loop(0, 2, body, 0)

    def p3_copies(u, to, at, frm):
        return (remote(c3.at[u, to], rc3.at[u, frm], s_3.at[u, 0, to], r_3.at[u, 0, frm], at),
                remote(m3.at[u, to], rm3.at[u, frm], s_3.at[u, 1, to], r_3.at[u, 1, frm], at))

    def column_code(v):
        return code_of(jnp.max(peak(v), axis=0, keepdims=True))

    def along_z(u):
        scales = {}
        for axis in range(2):
            me = (y, x)[axis]
            for k in range(1, 4):
                frm = wrap(me - k, 4)
                q = p2_copy(u, axis, wrap(me + k, 4), dev(dc=1), frm)
                pending.append(q)
                q.wait_recv()
                scales[axis, k] = scale_tile(rm2[u, axis, frm, pl.ds(128, 16)])

        def sum2(j, carry):
            for axis in range(2):
                me = (y, x)[axis]
                v = red[u, axis, me, j]
                for k in range(1, 4):
                    v = v + tile(wide(rm2[u, axis, wrap(me - k, 4), unit_rows(j)]).astype(F32)) * scales[axis, k]
                to = 4 * axis + j
                s_buf[u, to] = v
                code = column_code(v)
                c3[u, to] = code
                m3[u, to] = rounded(v, 1.0 / scale_of(code))

                @pl.when(z != to)
                def _():
                    for q in p3_copies(u, to, dev(dz=to - z), z):
                        q.start()

            return carry

        lax.fori_loop(0, 4, sum2, 0)

    def p4_copies(u, src, k):
        return (remote(gc[u].at[src], gc[u].at[src], s_4.at[u, 0, k - 1], r_4.at[u, 0, k - 1], dev(dz=k)),
                remote(gx[u].at[src], gx[u].at[src], s_4.at[u, 1, k - 1], r_4.at[u, 1, k - 1], dev(dz=k)))

    def gather_z(u):
        piece = s_buf[u, z]
        for k in range(1, NZ):
            for q in p3_copies(u, wrap(z + k, NZ), dev(dc=1), wrap(z - k, NZ)):
                pending.append(q)
                q.wait_recv()
        for k in range(1, NZ):
            frm = wrap(z - k, NZ)
            piece = piece + tile(wide(rm3[u, frm]).astype(F32)) * scale_of(rc3[u, frm])
        piece = piece * (1.0 / 256.0)
        code = column_code(piece)
        gc[u][z] = code
        gx[u][z] = rounded(piece, 1.0 / scale_of(code))
        for k in (4, 3, 5, 2, 6, 1, 7):
            begin(p4_copies(u, z, k))
        return piece

    def p5_copies(u, e):
        at = dev(dy=e // 4, dx=e % 4)
        return (remote(c5.at[u, e], rc5.at[u, e], s_5.at[u, 0, e], r_5.at[u, 0, e], at),
                remote(m5.at[u, e], rm5.at[u, e], s_5.at[u, 1, e], r_5.at[u, 1, e], at))

    def route(u):
        for k in range(1, NZ):
            for q in p4_copies(u, wrap(z - k, NZ), k):
                q.wait_recv()
        for i in (2, 1, 3, 0):
            for j in (2, 1, 3, 0):
                e = i * 4 + j
                which = local_j[wrap(x + j, NX) * SLOTS + wrap(y + i, NY)]
                take = jnp.maximum(which, 0)
                c5[u, e] = jnp.where(which >= 0, gc[u][take], jnp.zeros((1, 128), F32))
                m5[u, e] = jnp.where(which >= 0, wide(gx[u][take]), jnp.zeros((32, 128), jnp.int32)).astype(I16)
                if e:
                    begin(p5_copies(u, e))

    def half_copy(u, core):
        return remote(gq.at[y, core, u], gq.at[y, core, u], s_d.at[u], r_d.at[u], dev(dc=1))

    def open_half(slot, core, u):
        for i in range(NY):
            scale = scale_of(wide(gq[slot, core, u, i, pl.ds(32, 16)]).astype(F32)[0:1])
            v = tile(wide(gq[slot, core, u, i, pl.ds(0, 32)]).astype(F32)) * scale
            gbuf[i, core, :, pl.ds(u * 128, 128)] = v.reshape(32, 128)

    def collect(u):
        for i in range(NY):
            parts = [(m5[u, 0], c5[u, 0])] if i == 0 else []
            for j in range(NX):
                e = i * 4 + j
                if e:
                    for q in p5_copies(u, e):
                        q.wait_recv()
                    parts.append((rm5[u, e], rc5[u, e]))
            rows = [wide(v[0]) for v in parts]
            yi = wrap(y - i, NY)
            gq[y, c, u, yi, pl.ds(0, 32)] = ((rows[0] + rows[1]) + (rows[2] + rows[3])).astype(I16)
            code = (parts[0][1] + parts[1][1]) + (parts[2][1] + parts[3][1])
            gq[y, c, u, yi, pl.ds(32, 16)] = tail([code])
        begin([half_copy(u, c)])

    def rank_row(b, carry):
        ob = owner[b]
        total = jnp.int32(0)
        for e in range(NB):
            total = total + jnp.where((owner[e] == ob) & (e < b), 1, 0)
        rank[b] = total
        return carry

    def find(i, carry):
        target = lax.div(i, SLOTS) * NZ + z
        slot = lax.rem(i, SLOTS)
        found = jnp.int32(-1)
        for j in range(8):
            b = 4 * x + j if j < 4 else 16 + 4 * x + j - 4
            found = jnp.where((owner[b] == target) & (rank[b] == slot), j, found)
        local_j[i] = found
        return carry

    far(0)
    near(0)
    far(1)
    onward(0)
    near(1)
    owner_copy.wait()
    lax.fori_loop(0, NB, rank_row, 0)
    onward(1)
    last(0)
    last(1)
    along_z(0)
    along_z(1)
    lax.fori_loop(0, NX * SLOTS, find, 0)
    n_mine = jnp.int32(0)
    for b in range(NB):
        n_mine = n_mine + jnp.where(owner[b] == grp, 1, 0)
    pieces = [gather_z(u) for u in range(2)]
    route(0)
    route(1)
    collect(0)
    collect(1)
    g_square = jnp.sum(jnp.sum(pieces[0] * pieces[0] + pieces[1] * pieces[1], axis=0), axis=0, keepdims=True)

    def block_copies(slot, core, ssem, rsem, to):
        return [remote(gq.at[slot, core], gq.at[slot, core], ssem, rsem, to)]

    for k in (2, 1, 3):
        begin(block_copies(y, c, s_6.at[k - 1], r_6.at[k - 1], dev(dy=k)))
    stat_copy.wait()
    for u in range(2):
        open_half(y, c, u)
    for u in range(2):
        half_copy(u, oc).wait_recv()
        open_half(y, oc, u)

    def put_stats(slot, side, value):
        ns[slot, side] = jnp.where(n_mine > slot, value, stats[slot, side])

    def slot_stats(slot):
        for core in range(NC):
            for u in range(2):
                open_half(slot, core, u)
        g = gbuf[...].reshape(BS, BS)
        gp, gtp = split(g), split(g.T)
        put_stats(slot, 0, DECAY * stats[slot, 0] + dot3(gp, gtp))
        put_stats(slot, 1, DECAY * stats[slot, 1] + dot3(gtp, gp))

    g = gbuf[...].reshape(BS, BS)
    gt = g.T
    first, second = jnp.where(c == 0, g, gt), jnp.where(c == 0, gt, g)
    first_p, second_p = split(first), split(second)
    mat = DECAY * stats[y, c] + dot3(first_p, second_p)
    put_stats(y, c, mat)
    norm = jnp.sqrt(jnp.sum(jnp.sum(mat * mat, axis=0, keepdims=True), axis=1, keepdims=True))
    five = jnp.where(
        lax.broadcasted_iota(jnp.int32, (BS, BS), 0) == lax.broadcasted_iota(jnp.int32, (BS, BS), 1), 1.25, 0.0
    ).astype(F32)
    q0 = mat * (1.0 / norm)
    factor = five - 0.25 * q0
    xs[...] = factor * lax.rsqrt(jnp.sqrt(norm))

    def newton(i, carry):
        q = qs[...]
        fp = split(five - 0.25 * q)
        square = split(dot3(fp, fp))
        x_next = dot3(split(xs[...]), fp)
        qs[...] = dot3(split(dot3(square, square)), split(q))
        xs[...] = x_next
        return carry

    fp = split(factor)
    square = split(dot3(fp, fp))
    qs[...] = dot3(split(dot3(square, square)), split(q0))
    lax.fori_loop(0, ITERS - 3, newton, 0)
    q = qs[...]
    factor = five - 0.25 * q
    fp = split(factor)
    x5 = dot3(split(xs[...]), fp)
    square = split(dot3(fp, fp))
    fourth = dot3(square, square)
    xs[...] = 1.25 * x5 - 0.25 * dot3(split(fourth), split(dot3(split(q), split(x5))))

    root_copy = send(xs, xother, s_x, r_x, dev(dc=1))
    one_side = dot3(split(xs[...]), first_p)
    one_half = one_side.T[:, 128:]
    for k in (1, 2, 3):
        yk = wrap(y - k, NY)
        for q in block_copies(yk, c, s_6.at[k - 1], r_6.at[k - 1], dev(dy=k)):
            q.wait_recv()
        begin(block_copies(yk, c, s_7.at[k - 1], r_7.at[k - 1], dev(dc=1)))
    root_copy.wait_recv()
    other = xother[...]
    prec = dot3(
        split(jnp.where(c == 0, one_side, other)), split(jnp.where(c == 0, other[:, :128], one_half))
    ).reshape(32, 8, 128)
    p_square = jnp.sum(jnp.sum(prec * prec, axis=0), axis=0, keepdims=True)
    p_code = code_of(jnp.max(peak(prec), axis=0, keepdims=True))
    inverse = 1.0 / scale_of(p_code)
    end = jnp.concatenate([p_code] + sum_rows(g_square) + sum_rows(p_square) + [jnp.zeros((3, 128), F32)], axis=0)
    pbuf[...] = prec

    def pack_row(g):
        rows = (pbuf[g] * inverse + 12582912.0) - 12582912.0
        ma[g] = to16(jnp.concatenate([rows, end], axis=0))

    w = []
    for k in (4, 3, 5, 2, 6, 1, 7, 0):
        for j in (2, 1, 3, 0):
            e = j * 8 + k
            to = wrap(x + j, NX) * 8 + wrap(z + k, NZ)
            pack_row(to)
            if e:
                w.append(send(ma.at[to], rma.at[e], s_a.at[e], r_a.at[e], dev(dx=j, dz=k)))
    rma[0] = ma[grp]
    flush()
    put_stats(y, oc, DECAY * stats[y, oc] + dot3(second_p, first_p))

    def other_slot(k):
        yk = wrap(y - k, NY)
        for q in block_copies(yk, oc, s_7.at[k - 1], r_7.at[k - 1], dev(dc=1)):
            q.wait_recv()
        slot_stats(yk)

    def sums_of(end, at):
        return sums_from(end[at:at + 2]), sums_from(end[at + 2:at + 4])

    def add(pairs):
        while len(pairs) > 1:
            pairs = [(a[0] + b[0], a[1] + b[1]) for a, b in zip(pairs[::2], pairs[1::2])]
        return pairs[0]

    other_slot(1)
    for q in w:
        q.wait_recv()

    def pick(i, carry):
        pair = []
        for u in range(2):
            b = 2 * i + u
            o = owner[b]
            at = wrap(x - lax.div(o, NZ), NX) * 8 + wrap(z - lax.rem(o, NZ), NZ)
            pair.append(jnp.where(rank[b] == y, wide(rma[at]), jnp.zeros((16, 128), jnp.int32)))
            codes[pl.ds(lax.rem(b, 8), 1)] = pair[u][8:9].astype(F32)
        rows = jnp.concatenate([v[0:8] for v in pair], axis=0).astype(I16)
        my[lax.div(i, 4), pl.ds(pl.multiple_of(lax.rem(i, 4) * 16, 16), 16)] = rows
        return carry

    w = []
    for k in (2, 1, 3, 0):
        yy = wrap(y + k, NY)
        lax.fori_loop(4 * yy, 4 * yy + 4, pick, 0)
        my[yy, pl.ds(64, 16)] = tail([codes[...]])
        if k:
            w.append(send(my.at[yy], rmy.at[k], s_y.at[k], r_y.at[k], dev(dy=k)))
    g_sum, p_sum = add([sums_of(wide(rma[e]).astype(F32), 9) for e in range(NX * NZ)])
    flush()
    other_slot(2)
    for q in w:
        q.wait_recv()
    ends = [wide(v).astype(F32) for v in (my[y, pl.ds(64, 16)], rmy[1, pl.ds(64, 16)],
                                          rmy[2, pl.ds(64, 16)], rmy[3, pl.ds(64, 16)])]
    block_codes = (ends[0][0:8] + ends[1][0:8]) + (ends[2][0:8] + ends[3][0:8])
    fq[c, y, pl.ds(0, 64)] = (
        (wide(my[y, pl.ds(0, 64)]) + wide(rmy[1, pl.ds(0, 64)]))
        + (wide(rmy[2, pl.ds(0, 64)]) + wide(rmy[3, pl.ds(0, 64)]))
    ).astype(I16)
    fq[c, y, pl.ds(64, 16)] = tail([block_codes] + sum_rows(g_sum) + sum_rows(p_sum) + [jnp.zeros((4, 128), F32)])

    def ag_copy(core, yy, e, to):
        return remote(fq.at[core, yy], fq.at[core, yy], s_ag.at[e], r_ag.at[e], to)

    for k in (2, 1, 3, 0):
        for o in range(2):
            e = k * 2 + o
            if e:
                begin([ag_copy(c, y, e, dev(dy=k, dc=o))])
    other_slot(3)
    for k in range(NY):
        for o in range(2):
            e = k * 2 + o
            if e:
                ag_copy(wrap(c + o, 2), wrap(y - k, NY), e, dev(dy=k, dc=o)).wait_recv()
    g_sum, p_sum = add([sums_of(wide(fq[core, yy, pl.ds(64, 16)]).astype(F32), 8) for core in range(NC) for yy in range(NY)])
    ratio = jnp.sqrt(jnp.sum(g_sum, axis=1, keepdims=True) / jnp.sum(p_sum, axis=1, keepdims=True))
    ratio_ref[...] = jnp.broadcast_to(ratio, (1, 128))
    flush()


def hand_over(fq, ratio, ns_in, dir_out, ns_out, direction, sems):
    copies = []
    for i in range(SLOTS):
        for j in range(2):
            for half in range(2):
                at = (i, j, pl.ds(128 * half, 128))
                copies.append(pltpu.make_async_copy(ns_in.at[at], ns_out.at[at], sems.at[2 + len(copies)]))
    for q in copies:
        q.start()
    for half in range(2):
        for yy in (2 * half, 2 * half + 1):
            for h in range(NC):
                block_scales = scale_of(wide(fq[h, yy, pl.ds(64, 16)]).astype(F32)) * ratio[...]
                for i in range(8):
                    both = wide(fq[h, yy, pl.ds(16 * (i // 2), 16)]).astype(F32)
                    at = (yy * 8 + i) * 256 + h * 128
                    direction[:, pl.ds(at, 128)] = both[8 * (i % 2):8 * (i % 2) + 8] * block_scales[i:i + 1]
        at = (slice(None), pl.ds(4096 * half, 4096))
        copies.append(pltpu.make_async_copy(direction.at[at], dir_out.at[at], sems.at[half]))
        copies[-1].start()
    for q in copies:
        q.wait()


def local(grad_parts, stats, owner):
    grad = grad_parts.reshape(NY, NC, 32, 8192)
    vm, dma = pltpu.VMEM, pltpu.SemaphoreType.DMA
    t = (8, 128)
    scratch = [
        vm((SLOTS, 2, BS, BS), F32),
        vm((NY, 32, 8192), BF16), vm((NY, 32, 8192), BF16),
        vm((2, 2, 6, 272, 128), I16), vm((2, 2, 6, 272, 128), I16),
        vm((2, 2, 4, 4, 4) + t, F32),
        vm((2, 2, 4, 144, 128), I16), vm((2, 2, 4, 144, 128), I16),
        vm((2, 8, 4) + t, F32),
        vm((2, 8, 32, 128), I16), vm((2, 8, 32, 128), I16),
        vm((2, 8, 1, 128), F32), vm((2, 8, 1, 128), F32),
        vm((8, 32, 128), I16), vm((8, 32, 128), I16),
        vm((8, 1, 128), F32), vm((8, 1, 128), F32),
        vm((2, 16, 32, 128), I16), vm((2, 16, 32, 128), I16),
        vm((2, 16, 1, 128), F32), vm((2, 16, 1, 128), F32),
        vm((SLOTS, NC, 2, NY, 48, 128), I16),
        vm((NY, NC, 32, BS), F32),
        vm((8, 128), F32), vm((2, 4, 4) + t, F32),
        vm((BS, BS), F32), vm((BS, BS), F32), vm((BS, BS), F32),
        vm((32,) + t, F32), vm((32, 16, 128), I16), vm((32, 16, 128), I16),
        vm((NY, 80, 128), I16), vm((NY, 80, 128), I16),
        pltpu.SMEM((NB,), jnp.int32), pltpu.SMEM((NB,), jnp.int32), pltpu.SMEM((NX * SLOTS,), jnp.int32),
        dma, dma((10,)), dma, dma((10,)), dma((10,)), dma((2, 2, 6)), dma((2, 2, 6)),
        dma((2, 2, 4)), dma((2, 2, 4)), dma((2, 2, 8)), dma((2, 2, 8)), dma((2, 2, 7)), dma((2, 2, 7)),
        dma((2, 2, 16)), dma((2, 2, 16)),
        dma((2,)), dma((2,)), dma((3,)), dma((3,)), dma((3,)), dma((3,)), dma, dma,
        dma((32,)), dma((32,)), dma((4,)), dma((4,)), dma((8,)), dma((8,)),
    ]
    results = pl.pallas_call(
        kernel,
        out_shape=(pltpu.VMEM((NC, NY, 80, 128), I16), pltpu.VMEM((1, 128), F32), pltpu.VMEM((SLOTS, 2, BS, BS), F32)),
        in_specs=[
            pl.BlockSpec(memory_space=pltpu.HBM),
            pl.BlockSpec(memory_space=pltpu.HBM),
            pl.BlockSpec(memory_space=pltpu.HBM),
        ],
        out_specs=(pl.BlockSpec(memory_space=pltpu.VMEM),) * 3,
        scratch_shapes=scratch,
        compiler_params=pltpu.CompilerParams(
            collective_id=0, has_side_effects=True, vmem_limit_bytes=51 * 1024 * 1024
        ),
        cost_estimate=pl.CostEstimate(flops=4_000_000_000, bytes_accessed=9_000_000, transcendentals=0),
    )(*[pltpu.with_memory_space_constraint(v, pltpu.HBM) for v in (grad, stats, owner)])
    return pl.pallas_call(
        hand_over,
        out_shape=(
            jax.ShapeDtypeStruct((8, 8192), F32),
            jax.ShapeDtypeStruct((SLOTS, 2, BS, BS), F32),
        ),
        in_specs=[pl.BlockSpec(memory_space=pltpu.VMEM)] * 3,
        out_specs=(pl.BlockSpec(memory_space=pltpu.HBM), pl.BlockSpec(memory_space=pltpu.HBM)),
        scratch_shapes=[vm((8, 8192), F32), dma((2 + 4 * SLOTS,))],
    )(*[pltpu.with_memory_space_constraint(v, pltpu.VMEM) for v in results])


def solution(mesh):
    return jax.shard_map(
        local,
        mesh=mesh,
        in_specs=(P("rep", "grp", None, None), P("grp", None, None, None), P()),
        out_specs=(P("grp", None), P("grp", None, None, None)),
        check_vma=False,
    )
```

```python
import functools
import jax
import jax.numpy as jnp
from jax import lax
from jax.experimental import pallas as pl
from jax.experimental.pallas import tpu as pltpu
from jax.sharding import PartitionSpec as P

BS = 256
ITERS = 6
DECAY = 0.9
NX, NY, NZ, NC = 4, 4, 8, 2
NB, SLOTS = 32, 4
MESH = pl.DeviceIdType.MESH
F32, BF16, I16 = jnp.float32, jnp.bfloat16, jnp.int16
TOP = 32700.0


def split(a):
    hi = a.astype(BF16)
    return hi, (a - hi.astype(F32)).astype(BF16)


def dot3(a, b):
    rows = a[0].shape[0]
    both = jnp.dot(jnp.concatenate(a, axis=0), b[0], preferred_element_type=F32)
    return both[:rows] + (both[rows:] + jnp.dot(a[0], b[1], preferred_element_type=F32))


def scale_of(code):
    return jnp.exp2(code * 0.125) * (1.0 / TOP)


def code_of(top):
    return jnp.ceil(jnp.log2(jnp.maximum(top, 1e-30)) * 8.0)


def rounded(v, inverse):
    q = (v * inverse + 12582912.0) - 12582912.0
    return to16(q.reshape(v.shape[0] * 8, 128))


def peak(v):
    return jnp.max(jnp.abs(v), axis=0)


def narrow(v):
    code = code_of(jnp.max(peak(v), axis=0, keepdims=True))
    return rounded(v, 1.0 / scale_of(code)), code


def to16(v):
    return v.astype(jnp.int32).astype(I16)


def wide(q):
    return q.astype(jnp.int32)


def sum_rows(v):
    v = jnp.maximum(v, 1e-36)
    e = jnp.floor(jnp.log2(v))
    return [e, jnp.round((v * jnp.exp2(-e) - 1.0) * 16000.0)]


def sums_from(rows):
    return jnp.exp2(rows[0:1]) * (1.0 + rows[1:2] * (1.0 / 16000.0))


def tail(rows):
    left = 16 - sum(r.shape[0] for r in rows)
    zero = [jnp.zeros((left, 128), F32)] if left else []
    return to16(jnp.concatenate(list(rows) + zero, axis=0))


def kernel(
    grad, stats_hbm, owner_hbm,
    fq, ratio_ref, ns,
    stats, own, sib,
    m1, rm1, red, m2, rm2, s_buf, m3, rm3, c3, rc3, gx0, gx1, gc0, gc1, m5, rm5, c5, rc5, gq, gbuf, codes, acc,
    xs, qs, xother, ma, rma, my, rmy,
    owner, rank, local_j,
    s_owner, s_own, s_stat, s_sib, r_sib, s_1, r_1, s_2, r_2, s_3, r_3, s_4, r_4, s_5, r_5,
    s_d, r_d, s_6, r_6, s_7, r_7, s_x, r_x, s_a, r_a, s_y, r_y, s_ag, r_ag,
):
    gx, gc = (gx0, gx1), (gc0, gc1)
    rep, grp = lax.axis_index("rep"), lax.axis_index("grp")
    y, c = lax.div(rep, 2), lax.rem(rep, 2)
    x, z = lax.div(grp, 8), lax.rem(grp, 8)

    def wrap(v, n):
        return lax.rem(v + n, n)

    def dev(dy=0, dc=0, dx=0, dz=0):
        return (wrap(y + dy, NY) * 2 + wrap(c + dc, 2), wrap(x + dx, NX) * 8 + wrap(z + dz, NZ))

    pending = []

    def remote(src, dst, ssem, rsem, to):
        return pltpu.make_async_remote_copy(
            src_ref=src, dst_ref=dst, send_sem=ssem, recv_sem=rsem, device_id=to, device_id_type=MESH
        )

    def send(src, dst, ssem, rsem, to):
        copy = remote(src, dst, ssem, rsem, to)
        copy.start()
        pending.append(copy)
        return copy

    def flush():
        for q in pending:
            q.wait_send()
        pending.clear()

    def xcols(k):
        return pl.ds(pl.multiple_of(wrap(x + k, NX) * 1024, 1024), 1024)

    def chunk(axis, k, h, core=None):
        lead = () if core is None else (core,)
        if axis == 0:
            yy = pl.ds(0, 4) if h is None else pl.ds(2 * h, 2)
            return (yy,) + lead + (slice(None), xcols(k))
        cols = pl.ds(4096, 4096) if h is None else pl.ds(4096 + 2048 * h, 2048)
        return (wrap(y + k, NY),) + lead + (slice(None), cols)

    pieces_in_order = [(axis, k, h) for k, h in ((2, 0), (2, 1), (1, None), (-1, None), (0, None)) for axis in range(2)]
    def own_copy(i, axis, k, h):
        return pltpu.make_async_copy(grad.at[chunk(axis, k, h, c)], own.at[chunk(axis, k, h)], s_own.at[i])

    partners = [dict(dc=1)]
    partners += [dict(dx=j) for j in (1, -1, 2)] + [dict(dy=i) for i in (1, -1, 2)]
    partners += [dict(dz=k) for k in range(1, NZ)]
    barrier = pltpu.get_barrier_semaphore()
    for p in partners:
        pl.semaphore_signal(barrier, inc=1, device_id=dev(**p), device_id_type=MESH)
    for i, piece in enumerate(pieces_in_order):
        own_copy(i, *piece).start()
    owner_copy = pltpu.make_async_copy(owner_hbm, owner, s_owner)
    owner_copy.start()
    stat_copy = pltpu.make_async_copy(stats_hbm, stats, s_stat)
    stat_copy.start()

    pl.semaphore_wait(barrier, len(partners))

    oc = wrap(c + 1, 2)
    def sib_copy(i, axis, k, h):
        return remote(grad.at[chunk(axis, k, h, oc)], sib.at[chunk(axis, k, h)], s_sib.at[i], r_sib.at[i], dev(dc=1))

    def begin(copies):
        for q in copies:
            q.start()
            pending.append(q)

    for i, piece in enumerate(pieces_in_order):
        begin([sib_copy(i, *piece)])

    def ready(i, axis, k, h):
        own_copy(i, axis, k, h).wait()
        sib_copy(i, axis, k, h).wait_recv()

    def tile(v):
        return v.reshape(4, 8, 128)

    def unit(axis, k, h, a, b):
        if axis == 0:
            row, at = 2 * h + a, wrap(x + k, NX) * 1024 + b * 128
        else:
            row, at = wrap(y + k, NY), 4096 + 2048 * h + (a * 8 + b) * 128
        at = pl.ds(pl.multiple_of(at, 128), 128)
        return own[row, :, at].astype(F32) + sib[row, :, at].astype(F32)

    def unit_rows(n):
        return pl.ds(n * 32 if isinstance(n, int) else pl.multiple_of(n * 32, 32), 32)

    def scale_tile(rows):
        return scale_of(wide(rows).astype(F32)[0:8])

    def scale_tile(rows):
        return scale_of(wide(rows).astype(F32)[0:8])

    def part(u, axis, k, h, adds, flow):
        scales = [scale_tile(rm1[u, axis, f, pl.ds(256, 16)]) for f in adds]
        zero = jnp.zeros((8, 128), F32)
        tops = [zero, zero]
        for a in range(2):
            for i in range(4):
                v = tile(unit(axis, k, h, a, 2 * i + u))
                for f, scale in zip(adds, scales):
                    v = v + tile(wide(rm1[u, axis, f, unit_rows(4 * a + i)]).astype(F32)) * scale
                if flow is None:
                    red[u, axis, 2 * h + a, i] = v
                else:
                    acc[a, i] = v
                tops[a] = jnp.maximum(tops[a], peak(v))
        if flow is not None:
            tops = [jnp.maximum(tops[0], tops[1])] * 2
        codes = [code_of(t) for t in tops]
        inverse = [1.0 / scale_of(code) for code in codes]
        for a in range(2):
            for i in range(4):
                if flow is None:
                    m2[u, axis, 2 * h + a, unit_rows(i)] = rounded(red[u, axis, 2 * h + a, i], inverse[a])
                else:
                    m1[u, axis, flow, unit_rows(4 * a + i)] = rounded(acc[a, i], inverse[a])
            if flow is None:
                m2[u, axis, 2 * h + a, pl.ds(128, 16)] = tail([codes[a]])
        if flow is not None:
            m1[u, axis, flow, pl.ds(256, 16)] = tail([codes[0]])

    def flow_copy(u, axis, f, hop):
        to = dev(dx=hop) if axis == 0 else dev(dy=hop)
        return remote(m1.at[u, axis, f], rm1.at[u, axis, f], s_1.at[u, axis, f], r_1.at[u, axis, f], to)

    def arrived(u, axis, f):
        flow_copy(u, axis, f, 1).wait_recv()

    def far(u):
        def body(h, carry):
            for axis in range(2):
                if u == 0:
                    ready(2 * h + axis, axis, 2, h)
                part(u, axis, 2, h, [], h)
                flow_copy(u, axis, h, 1 - 2 * h).start()
            return carry

        lax.fori_loop(0, 2, body, 0)

    def near(u):
        def body(h, carry):
            hop = 2 * h - 1
            for axis in range(2):
                if u == 0:
                    ready(6 - 2 * h + axis, axis, hop, None)
                part(u, axis, hop, h, [], 2 + h)
                flow_copy(u, axis, 2 + h, hop).start()
            return carry

        lax.fori_loop(0, 2, body, 0)

    def onward(u):
        def body(h, carry):
            hop = 1 - 2 * h
            for axis in range(2):
                arrived(u, axis, h)
                part(u, axis, hop, h, [h], 4 + h)
                flow_copy(u, axis, 4 + h, hop).start()
            return carry

        lax.fori_loop(0, 2, body, 0)
        for axis in range(2):
            for f in range(6):
                pending.append(flow_copy(u, axis, f, 1))

    def p2_copy(u, axis, to, at, frm):
        return remote(m2.at[u, axis, to], rm2.at[u, axis, frm], s_2.at[u, axis, to], r_2.at[u, axis, frm], at)

    def p2_send(u, axis, to):
        me = (y, x)[axis]
        at = dev(dy=to - y) if axis == 0 else dev(dx=to - x)

        @pl.when(me != to)
        def _():
            p2_copy(u, axis, to, at, me).start()

    def last(u):
        def body(h, carry):
            for axis in range(2):
                arrived(u, axis, 2 + h)
                arrived(u, axis, 4 + h)
                part(u, axis, 0, h, [2 + h, 4 + h], None)
                p2_send(u, axis, 2 * h)
                p2_send(u, axis, 2 * h + 1)
            return carry

        if u == 0:
            for axis in range(2):
                ready(8 + axis, axis, 0, None)
        lax.fori_loop(0, 2, body, 0)

    def p3_copies(u, to, at, frm):
        return (remote(c3.at[u, to], rc3.at[u, frm], s_3.at[u, 0, to], r_3.at[u, 0, frm], at),
                remote(m3.at[u, to], rm3.at[u, frm], s_3.at[u, 1, to], r_3.at[u, 1, frm], at))

    def column_code(v):
        return code_of(jnp.max(peak(v), axis=0, keepdims=True))

    def along_z(u):
        scales = {}
        for axis in range(2):
            me = (y, x)[axis]
            for k in range(1, 4):
                frm = wrap(me - k, 4)
                q = p2_copy(u, axis, wrap(me + k, 4), dev(dc=1), frm)
                pending.append(q)
                q.wait_recv()
                scales[axis, k] = scale_tile(rm2[u, axis, frm, pl.ds(128, 16)])

        def sum2(j, carry):
            for axis in range(2):
                me = (y, x)[axis]
                v = red[u, axis, me, j]
                for k in range(1, 4):
                    v = v + tile(wide(rm2[u, axis, wrap(me - k, 4), unit_rows(j)]).astype(F32)) * scales[axis, k]
                to = 4 * axis + j
                s_buf[u, to] = v
                code = column_code(v)
                c3[u, to] = code
                m3[u, to] = rounded(v, 1.0 / scale_of(code))

                @pl.when(z != to)
                def _():
                    for q in p3_copies(u, to, dev(dz=to - z), z):
                        q.start()

            return carry

        lax.fori_loop(0, 4, sum2, 0)

    def p4_copies(u, src, k):
        return (remote(gc[u].at[src], gc[u].at[src], s_4.at[u, 0, k - 1], r_4.at[u, 0, k - 1], dev(dz=k)),
                remote(gx[u].at[src], gx[u].at[src], s_4.at[u, 1, k - 1], r_4.at[u, 1, k - 1], dev(dz=k)))

    def gather_z(u):
        piece = s_buf[u, z]
        for k in range(1, NZ):
            for q in p3_copies(u, wrap(z + k, NZ), dev(dc=1), wrap(z - k, NZ)):
                pending.append(q)
                q.wait_recv()
        for k in range(1, NZ):
            frm = wrap(z - k, NZ)
            piece = piece + tile(wide(rm3[u, frm]).astype(F32)) * scale_of(rc3[u, frm])
        piece = piece * (1.0 / 256.0)
        code = column_code(piece)
        gc[u][z] = code
        gx[u][z] = rounded(piece, 1.0 / scale_of(code))
        for k in (4, 3, 5, 2, 6, 1, 7):
            begin(p4_copies(u, z, k))
        return piece

    def p5_copies(u, e):
        at = dev(dy=e // 4, dx=e % 4)
        return (remote(c5.at[u, e], rc5.at[u, e], s_5.at[u, 0, e], r_5.at[u, 0, e], at),
                remote(m5.at[u, e], rm5.at[u, e], s_5.at[u, 1, e], r_5.at[u, 1, e], at))

    def route(u):
        for k in range(1, NZ):
            for q in p4_copies(u, wrap(z - k, NZ), k):
                q.wait_recv()
        for i in (2, 1, 3, 0):
            for j in (2, 1, 3, 0):
                e = i * 4 + j
                which = local_j[wrap(x + j, NX) * SLOTS + wrap(y + i, NY)]
                take = jnp.maximum(which, 0)
                c5[u, e] = jnp.where(which >= 0, gc[u][take], jnp.zeros((1, 128), F32))
                m5[u, e] = jnp.where(which >= 0, wide(gx[u][take]), jnp.zeros((32, 128), jnp.int32)).astype(I16)
                if e:
                    begin(p5_copies(u, e))

    def half_copy(u, core):
        return remote(gq.at[y, core, u], gq.at[y, core, u], s_d.at[u], r_d.at[u], dev(dc=1))

    def open_half(slot, core, u):
        for i in range(NY):
            scale = scale_of(wide(gq[slot, core, u, i, pl.ds(32, 16)]).astype(F32)[0:1])
            v = tile(wide(gq[slot, core, u, i, pl.ds(0, 32)]).astype(F32)) * scale
            gbuf[i, core, :, pl.ds(u * 128, 128)] = v.reshape(32, 128)

    def collect(u):
        for i in range(NY):
            parts = [(m5[u, 0], c5[u, 0])] if i == 0 else []
            for j in range(NX):
                e = i * 4 + j
                if e:
                    for q in p5_copies(u, e):
                        q.wait_recv()
                    parts.append((rm5[u, e], rc5[u, e]))
            rows = [wide(v[0]) for v in parts]
            yi = wrap(y - i, NY)
            gq[y, c, u, yi, pl.ds(0, 32)] = ((rows[0] + rows[1]) + (rows[2] + rows[3])).astype(I16)
            code = (parts[0][1] + parts[1][1]) + (parts[2][1] + parts[3][1])
            gq[y, c, u, yi, pl.ds(32, 16)] = tail([code])
        begin([half_copy(u, c)])

    def rank_row(b, carry):
        ob = owner[b]
        total = jnp.int32(0)
        for e in range(NB):
            total = total + jnp.where((owner[e] == ob) & (e < b), 1, 0)
        rank[b] = total
        return carry

    def find(i, carry):
        target = lax.div(i, SLOTS) * NZ + z
        slot = lax.rem(i, SLOTS)
        found = jnp.int32(-1)
        for j in range(8):
            b = 4 * x + j if j < 4 else 16 + 4 * x + j - 4
            found = jnp.where((owner[b] == target) & (rank[b] == slot), j, found)
        local_j[i] = found
        return carry

    far(0)
    near(0)
    far(1)
    onward(0)
    near(1)
    owner_copy.wait()
    lax.fori_loop(0, NB, rank_row, 0)
    onward(1)
    last(0)
    last(1)
    along_z(0)
    along_z(1)
    lax.fori_loop(0, NX * SLOTS, find, 0)
    n_mine = jnp.int32(0)
    for b in range(NB):
        n_mine = n_mine + jnp.where(owner[b] == grp, 1, 0)
    pieces = [gather_z(u) for u in range(2)]
    route(0)
    route(1)
    collect(0)
    collect(1)
    g_square = jnp.sum(jnp.sum(pieces[0] * pieces[0] + pieces[1] * pieces[1], axis=0), axis=0, keepdims=True)

    def block_copies(slot, core, ssem, rsem, to):
        return [remote(gq.at[slot, core], gq.at[slot, core], ssem, rsem, to)]

    for k in (2, 1, 3):
        begin(block_copies(y, c, s_6.at[k - 1], r_6.at[k - 1], dev(dy=k)))
    stat_copy.wait()
    for u in range(2):
        open_half(y, c, u)
    for u in range(2):
        half_copy(u, oc).wait_recv()
        open_half(y, oc, u)

    def put_stats(slot, side, value):
        ns[slot, side] = jnp.where(n_mine > slot, value, stats[slot, side])

    def slot_stats(slot):
        for core in range(NC):
            for u in range(2):
                open_half(slot, core, u)
        g = gbuf[...].reshape(BS, BS)
        gp, gtp = split(g), split(g.T)
        put_stats(slot, 0, DECAY * stats[slot, 0] + dot3(gp, gtp))
        put_stats(slot, 1, DECAY * stats[slot, 1] + dot3(gtp, gp))

    g = gbuf[...].reshape(BS, BS)
    gt = g.T
    first, second = jnp.where(c == 0, g, gt), jnp.where(c == 0, gt, g)
    first_p, second_p = split(first), split(second)
    mat = DECAY * stats[y, c] + dot3(first_p, second_p)
    put_stats(y, c, mat)
    norm = jnp.sqrt(jnp.sum(jnp.sum(mat * mat, axis=0, keepdims=True), axis=1, keepdims=True))
    five = jnp.where(
        lax.broadcasted_iota(jnp.int32, (BS, BS), 0) == lax.broadcasted_iota(jnp.int32, (BS, BS), 1), 1.25, 0.0
    ).astype(F32)
    q0 = mat * (1.0 / norm)
    factor = five - 0.25 * q0
    xs[...] = factor * lax.rsqrt(jnp.sqrt(norm))

    def newton(i, carry):
        q = qs[...]
        fp = split(five - 0.25 * q)
        square = split(dot3(fp, fp))
        x_next = dot3(split(xs[...]), fp)
        qs[...] = dot3(split(dot3(square, square)), split(q))
        xs[...] = x_next
        return carry

    fp = split(factor)
    square = split(dot3(fp, fp))
    qs[...] = dot3(split(dot3(square, square)), split(q0))
    lax.fori_loop(0, ITERS - 3, newton, 0)
    q = qs[...]
    factor = five - 0.25 * q
    fp = split(factor)
    x5 = dot3(split(xs[...]), fp)
    square = split(dot3(fp, fp))
    fourth = dot3(square, square)
    xs[...] = 1.25 * x5 - 0.25 * dot3(split(fourth), split(dot3(split(q), split(x5))))

    root_copy = send(xs, xother, s_x, r_x, dev(dc=1))
    one_side = dot3(split(xs[...]), first_p)
    one_half = one_side.T[:, 128:]
    for k in (1, 2, 3):
        yk = wrap(y - k, NY)
        for q in block_copies(yk, c, s_6.at[k - 1], r_6.at[k - 1], dev(dy=k)):
            q.wait_recv()
        begin(block_copies(yk, c, s_7.at[k - 1], r_7.at[k - 1], dev(dc=1)))
    root_copy.wait_recv()
    other = xother[...]
    prec = dot3(
        split(jnp.where(c == 0, one_side, other)), split(jnp.where(c == 0, other[:, :128], one_half))
    ).reshape(32, 8, 128)
    p_square = jnp.sum(jnp.sum(prec * prec, axis=0), axis=0, keepdims=True)
    p_code = code_of(jnp.max(peak(prec), axis=0, keepdims=True))
    inverse = 1.0 / scale_of(p_code)
    end = jnp.concatenate([p_code] + sum_rows(g_square) + sum_rows(p_square) + [jnp.zeros((3, 128), F32)], axis=0)
    for i in range(NX * NZ):
        rows = (prec[i] * inverse + 12582912.0) - 12582912.0
        ma[i] = to16(jnp.concatenate([rows, end], axis=0))

    w = []
    for k in (4, 3, 5, 2, 6, 1, 7, 0):
        for j in (2, 1, 3, 0):
            if k or j:
                e = j * 8 + k
                w.append(send(ma.at[wrap(x + j, NX) * 8 + wrap(z + k, NZ)], rma.at[e], s_a.at[e], r_a.at[e], dev(dx=j, dz=k)))
    rma[0] = ma[grp]
    flush()
    put_stats(y, oc, DECAY * stats[y, oc] + dot3(second_p, first_p))

    def other_slot(k):
        yk = wrap(y - k, NY)
        for q in block_copies(yk, oc, s_7.at[k - 1], r_7.at[k - 1], dev(dc=1)):
            q.wait_recv()
        slot_stats(yk)

    def sums_of(end, at):
        return sums_from(end[at:at + 2]), sums_from(end[at + 2:at + 4])

    def add(pairs):
        while len(pairs) > 1:
            pairs = [(a[0] + b[0], a[1] + b[1]) for a, b in zip(pairs[::2], pairs[1::2])]
        return pairs[0]

    other_slot(1)
    other_slot(2)
    for q in w:
        q.wait_recv()

    def pick(i, carry):
        pair = []
        for u in range(2):
            b = 2 * i + u
            o = owner[b]
            at = wrap(x - lax.div(o, NZ), NX) * 8 + wrap(z - lax.rem(o, NZ), NZ)
            pair.append(jnp.where(rank[b] == y, wide(rma[at]), jnp.zeros((16, 128), jnp.int32)))
            codes[pl.ds(lax.rem(b, 8), 1)] = pair[u][8:9].astype(F32)
        rows = jnp.concatenate([v[0:8] for v in pair], axis=0).astype(I16)
        my[lax.div(i, 4), pl.ds(pl.multiple_of(lax.rem(i, 4) * 16, 16), 16)] = rows
        return carry

    w = []
    for k in (2, 1, 3, 0):
        yy = wrap(y + k, NY)
        lax.fori_loop(4 * yy, 4 * yy + 4, pick, 0)
        my[yy, pl.ds(64, 16)] = tail([codes[...]])
        if k:
            w.append(send(my.at[yy], rmy.at[k], s_y.at[k], r_y.at[k], dev(dy=k)))
    g_sum, p_sum = add([sums_of(wide(rma[e]).astype(F32), 9) for e in range(NX * NZ)])
    flush()
    for q in w:
        q.wait_recv()
    ends = [wide(v).astype(F32) for v in (my[y, pl.ds(64, 16)], rmy[1, pl.ds(64, 16)],
                                          rmy[2, pl.ds(64, 16)], rmy[3, pl.ds(64, 16)])]
    block_codes = (ends[0][0:8] + ends[1][0:8]) + (ends[2][0:8] + ends[3][0:8])
    fq[c, y, pl.ds(0, 64)] = (
        (wide(my[y, pl.ds(0, 64)]) + wide(rmy[1, pl.ds(0, 64)]))
        + (wide(rmy[2, pl.ds(0, 64)]) + wide(rmy[3, pl.ds(0, 64)]))
    ).astype(I16)
    fq[c, y, pl.ds(64, 16)] = tail([block_codes] + sum_rows(g_sum) + sum_rows(p_sum) + [jnp.zeros((4, 128), F32)])

    def ag_copy(core, yy, e, to):
        return remote(fq.at[core, yy], fq.at[core, yy], s_ag.at[e], r_ag.at[e], to)

    for k in (2, 1, 3, 0):
        for o in range(2):
            e = k * 2 + o
            if e:
                begin([ag_copy(c, y, e, dev(dy=k, dc=o))])
    other_slot(3)
    for k in range(NY):
        for o in range(2):
            e = k * 2 + o
            if e:
                ag_copy(wrap(c + o, 2), wrap(y - k, NY), e, dev(dy=k, dc=o)).wait_recv()
    g_sum, p_sum = add([sums_of(wide(fq[core, yy, pl.ds(64, 16)]).astype(F32), 8) for core in range(NC) for yy in range(NY)])
    ratio = jnp.sqrt(jnp.sum(g_sum, axis=1, keepdims=True) / jnp.sum(p_sum, axis=1, keepdims=True))
    ratio_ref[...] = jnp.broadcast_to(ratio, (1, 128))
    flush()


def hand_over(fq, ratio, ns_in, dir_out, ns_out, direction, sems):
    copies = []
    for i in range(SLOTS):
        for j in range(2):
            for half in range(2):
                at = (i, j, pl.ds(128 * half, 128))
                copies.append(pltpu.make_async_copy(ns_in.at[at], ns_out.at[at], sems.at[2 + len(copies)]))
    for q in copies:
        q.start()
    for half in range(2):
        for yy in (2 * half, 2 * half + 1):
            for h in range(NC):
                block_scales = scale_of(wide(fq[h, yy, pl.ds(64, 16)]).astype(F32)) * ratio[...]
                for i in range(8):
                    both = wide(fq[h, yy, pl.ds(16 * (i // 2), 16)]).astype(F32)
                    at = (yy * 8 + i) * 256 + h * 128
                    direction[:, pl.ds(at, 128)] = both[8 * (i % 2):8 * (i % 2) + 8] * block_scales[i:i + 1]
        at = (slice(None), pl.ds(4096 * half, 4096))
        copies.append(pltpu.make_async_copy(direction.at[at], dir_out.at[at], sems.at[half]))
        copies[-1].start()
    for q in copies:
        q.wait()


def local(grad_parts, stats, owner):
    grad = grad_parts.reshape(NY, NC, 32, 8192)
    vm, dma = pltpu.VMEM, pltpu.SemaphoreType.DMA
    t = (8, 128)
    scratch = [
        vm((SLOTS, 2, BS, BS), F32),
        vm((NY, 32, 8192), BF16), vm((NY, 32, 8192), BF16),
        vm((2, 2, 6, 272, 128), I16), vm((2, 2, 6, 272, 128), I16),
        vm((2, 2, 4, 4, 4) + t, F32),
        vm((2, 2, 4, 144, 128), I16), vm((2, 2, 4, 144, 128), I16),
        vm((2, 8, 4) + t, F32),
        vm((2, 8, 32, 128), I16), vm((2, 8, 32, 128), I16),
        vm((2, 8, 1, 128), F32), vm((2, 8, 1, 128), F32),
        vm((8, 32, 128), I16), vm((8, 32, 128), I16),
        vm((8, 1, 128), F32), vm((8, 1, 128), F32),
        vm((2, 16, 32, 128), I16), vm((2, 16, 32, 128), I16),
        vm((2, 16, 1, 128), F32), vm((2, 16, 1, 128), F32),
        vm((SLOTS, NC, 2, NY, 48, 128), I16),
        vm((NY, NC, 32, BS), F32),
        vm((8, 128), F32), vm((2, 4, 4) + t, F32),
        vm((BS, BS), F32), vm((BS, BS), F32), vm((BS, BS), F32),
        vm((32, 16, 128), I16), vm((32, 16, 128), I16),
        vm((NY, 80, 128), I16), vm((NY, 80, 128), I16),
        pltpu.SMEM((NB,), jnp.int32), pltpu.SMEM((NB,), jnp.int32), pltpu.SMEM((NX * SLOTS,), jnp.int32),
        dma, dma((10,)), dma, dma((10,)), dma((10,)), dma((2, 2, 6)), dma((2, 2, 6)),
        dma((2, 2, 4)), dma((2, 2, 4)), dma((2, 2, 8)), dma((2, 2, 8)), dma((2, 2, 7)), dma((2, 2, 7)),
        dma((2, 2, 16)), dma((2, 2, 16)),
        dma((2,)), dma((2,)), dma((3,)), dma((3,)), dma((3,)), dma((3,)), dma, dma,
        dma((32,)), dma((32,)), dma((4,)), dma((4,)), dma((8,)), dma((8,)),
    ]
    results = pl.pallas_call(
        kernel,
        out_shape=(pltpu.VMEM((NC, NY, 80, 128), I16), pltpu.VMEM((1, 128), F32), pltpu.VMEM((SLOTS, 2, BS, BS), F32)),
        in_specs=[
            pl.BlockSpec(memory_space=pltpu.HBM),
            pl.BlockSpec(memory_space=pltpu.HBM),
            pl.BlockSpec(memory_space=pltpu.HBM),
        ],
        out_specs=(pl.BlockSpec(memory_space=pltpu.VMEM),) * 3,
        scratch_shapes=scratch,
        compiler_params=pltpu.CompilerParams(
            collective_id=0, has_side_effects=True, vmem_limit_bytes=51 * 1024 * 1024
        ),
        cost_estimate=pl.CostEstimate(flops=4_000_000_000, bytes_accessed=9_000_000, transcendentals=0),
    )(*[pltpu.with_memory_space_constraint(v, pltpu.HBM) for v in (grad, stats, owner)])
    return pl.pallas_call(
        hand_over,
        out_shape=(
            jax.ShapeDtypeStruct((8, 8192), F32),
            jax.ShapeDtypeStruct((SLOTS, 2, BS, BS), F32),
        ),
        in_specs=[pl.BlockSpec(memory_space=pltpu.VMEM)] * 3,
        out_specs=(pl.BlockSpec(memory_space=pltpu.HBM), pl.BlockSpec(memory_space=pltpu.HBM)),
        scratch_shapes=[vm((8, 8192), F32), dma((2 + 4 * SLOTS,))],
    )(*[pltpu.with_memory_space_constraint(v, pltpu.VMEM) for v in results])


def solution(mesh):
    return jax.shard_map(
        local,
        mesh=mesh,
        in_specs=(P("rep", "grp", None, None), P("grp", None, None, None), P()),
        out_specs=(P("grp", None), P("grp", None, None, None)),
        check_vma=False,
    )
```

```python
import functools
import jax
import jax.numpy as jnp
from jax import lax
from jax.experimental import pallas as pl
from jax.experimental.pallas import tpu as pltpu
from jax.sharding import PartitionSpec as P

BS = 256
ITERS = 6
DECAY = 0.9
NX, NY, NZ, NC = 4, 4, 8, 2
NB, SLOTS = 32, 4
MESH = pl.DeviceIdType.MESH
F32, BF16, I16 = jnp.float32, jnp.bfloat16, jnp.int16
TOP = 32700.0


def split(a):
    hi = a.astype(BF16)
    return hi, (a - hi.astype(F32)).astype(BF16)


def dot3(a, b):
    rows = a[0].shape[0]
    both = jnp.dot(jnp.concatenate(a, axis=0), b[0], preferred_element_type=F32)
    return both[:rows] + (both[rows:] + jnp.dot(a[0], b[1], preferred_element_type=F32))


def scale_of(code):
    return jnp.exp2(code * 0.125) * (1.0 / TOP)


def code_of(top):
    return jnp.ceil(jnp.log2(jnp.maximum(top, 1e-30)) * 8.0)


def rounded(v, inverse):
    q = (v * inverse + 12582912.0) - 12582912.0
    return to16(q.reshape(v.shape[0] * 8, 128))


def peak(v):
    return jnp.max(jnp.abs(v), axis=0)


def narrow(v):
    code = code_of(jnp.max(peak(v), axis=0, keepdims=True))
    return rounded(v, 1.0 / scale_of(code)), code


def to16(v):
    return v.astype(jnp.int32).astype(I16)


def wide(q):
    return q.astype(jnp.int32)


def sum_rows(v):
    v = jnp.maximum(v, 1e-36)
    e = jnp.floor(jnp.log2(v))
    return [e, jnp.round((v * jnp.exp2(-e) - 1.0) * 16000.0)]


def sums_from(rows):
    return jnp.exp2(rows[0:1]) * (1.0 + rows[1:2] * (1.0 / 16000.0))


def tail(rows):
    left = 16 - sum(r.shape[0] for r in rows)
    zero = [jnp.zeros((left, 128), F32)] if left else []
    return to16(jnp.concatenate(list(rows) + zero, axis=0))


def kernel(
    grad, stats_hbm, owner_hbm,
    fq, ratio_ref, ns,
    stats, own, sib,
    m1, rm1, red, m2, rm2, s_buf, m3, rm3, c3, rc3, gx0, gx1, gc0, gc1, m5, rm5, c5, rc5, gq, gbuf, codes, acc,
    xs, qs, xother, ma, rma, my, rmy,
    owner, rank, local_j,
    s_owner, s_own, s_stat, s_sib, r_sib, s_1, r_1, s_2, r_2, s_3, r_3, s_4, r_4, s_5, r_5,
    s_d, r_d, s_6, r_6, s_7, r_7, s_x, r_x, s_a, r_a, s_y, r_y, s_ag, r_ag,
):
    gx, gc = (gx0, gx1), (gc0, gc1)
    rep, grp = lax.axis_index("rep"), lax.axis_index("grp")
    y, c = lax.div(rep, 2), lax.rem(rep, 2)
    x, z = lax.div(grp, 8), lax.rem(grp, 8)

    def wrap(v, n):
        return lax.rem(v + n, n)

    def dev(dy=0, dc=0, dx=0, dz=0):
        return (wrap(y + dy, NY) * 2 + wrap(c + dc, 2), wrap(x + dx, NX) * 8 + wrap(z + dz, NZ))

    pending = []

    def remote(src, dst, ssem, rsem, to):
        return pltpu.make_async_remote_copy(
            src_ref=src, dst_ref=dst, send_sem=ssem, recv_sem=rsem, device_id=to, device_id_type=MESH
        )

    def send(src, dst, ssem, rsem, to):
        copy = remote(src, dst, ssem, rsem, to)
        copy.start()
        pending.append(copy)
        return copy

    def flush():
        for q in pending:
            q.wait_send()
        pending.clear()

    def xcols(k):
        return pl.ds(pl.multiple_of(wrap(x + k, NX) * 1024, 1024), 1024)

    def chunk(axis, k, h, core=None):
        lead = () if core is None else (core,)
        if axis == 0:
            yy = pl.ds(0, 4) if h is None else pl.ds(2 * h, 2)
            return (yy,) + lead + (slice(None), xcols(k))
        cols = pl.ds(4096, 4096) if h is None else pl.ds(4096 + 2048 * h, 2048)
        return (wrap(y + k, NY),) + lead + (slice(None), cols)

    pieces_in_order = [(axis, k, h) for k, h in ((2, 0), (2, 1), (1, None), (-1, None), (0, None)) for axis in range(2)]
    def own_copy(i, axis, k, h):
        return pltpu.make_async_copy(grad.at[chunk(axis, k, h, c)], own.at[chunk(axis, k, h)], s_own.at[i])

    partners = [dict(dc=1)]
    partners += [dict(dx=j) for j in (1, -1, 2)] + [dict(dy=i) for i in (1, -1, 2)]
    partners += [dict(dz=k) for k in range(1, NZ)]
    barrier = pltpu.get_barrier_semaphore()
    for p in partners:
        pl.semaphore_signal(barrier, inc=1, device_id=dev(**p), device_id_type=MESH)
    for i, piece in enumerate(pieces_in_order):
        own_copy(i, *piece).start()
    owner_copy = pltpu.make_async_copy(owner_hbm, owner, s_owner)
    owner_copy.start()
    stat_copy = pltpu.make_async_copy(stats_hbm, stats, s_stat)
    stat_copy.start()

    pl.semaphore_wait(barrier, len(partners))

    oc = wrap(c + 1, 2)
    def sib_copy(i, axis, k, h):
        return remote(grad.at[chunk(axis, k, h, oc)], sib.at[chunk(axis, k, h)], s_sib.at[i], r_sib.at[i], dev(dc=1))

    def begin(copies):
        for q in copies:
            q.start()
            pending.append(q)

    for i, piece in enumerate(pieces_in_order):
        begin([sib_copy(i, *piece)])

    def ready(i, axis, k, h):
        own_copy(i, axis, k, h).wait()
        sib_copy(i, axis, k, h).wait_recv()

    def tile(v):
        return v.reshape(4, 8, 128)

    def unit(axis, k, h, a, b):
        if axis == 0:
            row, at = 2 * h + a, wrap(x + k, NX) * 1024 + b * 128
        else:
            row, at = wrap(y + k, NY), 4096 + 2048 * h + (a * 8 + b) * 128
        at = pl.ds(pl.multiple_of(at, 128), 128)
        return own[row, :, at].astype(F32) + sib[row, :, at].astype(F32)

    def unit_rows(n):
        return pl.ds(n * 32 if isinstance(n, int) else pl.multiple_of(n * 32, 32), 32)

    def scale_tile(rows):
        return scale_of(wide(rows).astype(F32)[0:8])

    def scale_tile(rows):
        return scale_of(wide(rows).astype(F32)[0:8])

    def part(u, axis, k, h, adds, flow):
        scales = [scale_tile(rm1[u, axis, f, pl.ds(256, 16)]) for f in adds]
        zero = jnp.zeros((8, 128), F32)
        tops = [zero, zero]
        for a in range(2):
            for i in range(4):
                v = tile(unit(axis, k, h, a, 2 * i + u))
                for f, scale in zip(adds, scales):
                    v = v + tile(wide(rm1[u, axis, f, unit_rows(4 * a + i)]).astype(F32)) * scale
                if flow is None:
                    red[u, axis, 2 * h + a, i] = v
                else:
                    acc[a, i] = v
                tops[a] = jnp.maximum(tops[a], peak(v))
        if flow is not None:
            tops = [jnp.maximum(tops[0], tops[1])] * 2
        codes = [code_of(t) for t in tops]
        inverse = [1.0 / scale_of(code) for code in codes]
        for a in range(2):
            for i in range(4):
                if flow is None:
                    m2[u, axis, 2 * h + a, unit_rows(i)] = rounded(red[u, axis, 2 * h + a, i], inverse[a])
                else:
                    m1[u, axis, flow, unit_rows(4 * a + i)] = rounded(acc[a, i], inverse[a])
            if flow is None:
                m2[u, axis, 2 * h + a, pl.ds(128, 16)] = tail([codes[a]])
        if flow is not None:
            m1[u, axis, flow, pl.ds(256, 16)] = tail([codes[0]])

    def flow_copy(u, axis, f, hop):
        to = dev(dx=hop) if axis == 0 else dev(dy=hop)
        return remote(m1.at[u, axis, f], rm1.at[u, axis, f], s_1.at[u, axis, f], r_1.at[u, axis, f], to)

    def arrived(u, axis, f):
        flow_copy(u, axis, f, 1).wait_recv()

    def far(u):
        def body(h, carry):
            for axis in range(2):
                if u == 0:
                    ready(2 * h + axis, axis, 2, h)
                part(u, axis, 2, h, [], h)
                flow_copy(u, axis, h, 1 - 2 * h).start()
            return carry

        lax.fori_loop(0, 2, body, 0)

    def near(u):
        def body(h, carry):
            hop = 2 * h - 1
            for axis in range(2):
                if u == 0:
                    ready(6 - 2 * h + axis, axis, hop, None)
                part(u, axis, hop, h, [], 2 + h)
                flow_copy(u, axis, 2 + h, hop).start()
            return carry

        lax.fori_loop(0, 2, body, 0)

    def onward(u):
        def body(h, carry):
            hop = 1 - 2 * h
            for axis in range(2):
                arrived(u, axis, h)
                part(u, axis, hop, h, [h], 4 + h)
                flow_copy(u, axis, 4 + h, hop).start()
            return carry

        lax.fori_loop(0, 2, body, 0)
        for axis in range(2):
            for f in range(6):
                pending.append(flow_copy(u, axis, f, 1))

    def p2_copy(u, axis, to, at, frm):
        return remote(m2.at[u, axis, to], rm2.at[u, axis, frm], s_2.at[u, axis, to], r_2.at[u, axis, frm], at)

    def p2_send(u, axis, to):
        me = (y, x)[axis]
        at = dev(dy=to - y) if axis == 0 else dev(dx=to - x)

        @pl.when(me != to)
        def _():
            p2_copy(u, axis, to, at, me).start()

    def last(u):
        def body(h, carry):
            for axis in range(2):
                arrived(u, axis, 2 + h)
                arrived(u, axis, 4 + h)
                part(u, axis, 0, h, [2 + h, 4 + h], None)
                p2_send(u, axis, 2 * h)
                p2_send(u, axis, 2 * h + 1)
            return carry

        if u == 0:
            for axis in range(2):
                ready(8 + axis, axis, 0, None)
        lax.fori_loop(0, 2, body, 0)

    def p3_copies(u, to, at, frm):
        return (remote(c3.at[u, to], rc3.at[u, frm], s_3.at[u, 0, to], r_3.at[u, 0, frm], at),
                remote(m3.at[u, to], rm3.at[u, frm], s_3.at[u, 1, to], r_3.at[u, 1, frm], at))

    def column_code(v):
        return code_of(jnp.max(peak(v), axis=0, keepdims=True))

    def along_z(u):
        scales = {}
        for axis in range(2):
            me = (y, x)[axis]
            for k in range(1, 4):
                frm = wrap(me - k, 4)
                q = p2_copy(u, axis, wrap(me + k, 4), dev(dc=1), frm)
                pending.append(q)
                q.wait_recv()
                scales[axis, k] = scale_tile(rm2[u, axis, frm, pl.ds(128, 16)])

        def sum2(j, carry):
            for axis in range(2):
                me = (y, x)[axis]
                v = red[u, axis, me, j]
                for k in range(1, 4):
                    v = v + tile(wide(rm2[u, axis, wrap(me - k, 4), unit_rows(j)]).astype(F32)) * scales[axis, k]
                to = 4 * axis + j
                s_buf[u, to] = v
                code = column_code(v)
                c3[u, to] = code
                m3[u, to] = rounded(v, 1.0 / scale_of(code))

                @pl.when(z != to)
                def _():
                    for q in p3_copies(u, to, dev(dz=to - z), z):
                        q.start()

            return carry

        lax.fori_loop(0, 4, sum2, 0)

    def p4_copies(u, src, k):
        return (remote(gc[u].at[src], gc[u].at[src], s_4.at[u, 0, k - 1], r_4.at[u, 0, k - 1], dev(dz=k)),
                remote(gx[u].at[src], gx[u].at[src], s_4.at[u, 1, k - 1], r_4.at[u, 1, k - 1], dev(dz=k)))

    def gather_z(u):
        piece = s_buf[u, z]
        for k in range(1, NZ):
            for q in p3_copies(u, wrap(z + k, NZ), dev(dc=1), wrap(z - k, NZ)):
                pending.append(q)
                q.wait_recv()
        for k in range(1, NZ):
            frm = wrap(z - k, NZ)
            piece = piece + tile(wide(rm3[u, frm]).astype(F32)) * scale_of(rc3[u, frm])
        piece = piece * (1.0 / 256.0)
        code = column_code(piece)
        gc[u][z] = code
        gx[u][z] = rounded(piece, 1.0 / scale_of(code))
        for k in (4, 3, 5, 2, 6, 1, 7):
            begin(p4_copies(u, z, k))
        return piece

    def p5_copies(u, e):
        at = dev(dy=e // 4, dx=e % 4)
        return (remote(c5.at[u, e], rc5.at[u, e], s_5.at[u, 0, e], r_5.at[u, 0, e], at),
                remote(m5.at[u, e], rm5.at[u, e], s_5.at[u, 1, e], r_5.at[u, 1, e], at))

    def route(u):
        for k in range(1, NZ):
            for q in p4_copies(u, wrap(z - k, NZ), k):
                q.wait_recv()
        for i in (2, 1, 3, 0):
            for j in (2, 1, 3, 0):
                e = i * 4 + j
                which = local_j[wrap(x + j, NX) * SLOTS + wrap(y + i, NY)]
                take = jnp.maximum(which, 0)
                c5[u, e] = jnp.where(which >= 0, gc[u][take], jnp.zeros((1, 128), F32))
                m5[u, e] = jnp.where(which >= 0, wide(gx[u][take]), jnp.zeros((32, 128), jnp.int32)).astype(I16)
                if e:
                    begin(p5_copies(u, e))

    def half_copy(u, core):
        return remote(gq.at[y, core, u], gq.at[y, core, u], s_d.at[u], r_d.at[u], dev(dc=1))

    def open_half(slot, core, u):
        for i in range(NY):
            scale = scale_of(wide(gq[slot, core, u, i, pl.ds(32, 16)]).astype(F32)[0:1])
            v = tile(wide(gq[slot, core, u, i, pl.ds(0, 32)]).astype(F32)) * scale
            gbuf[i, core, :, pl.ds(u * 128, 128)] = v.reshape(32, 128)

    def collect(u):
        for i in range(NY):
            parts = [(m5[u, 0], c5[u, 0])] if i == 0 else []
            for j in range(NX):
                e = i * 4 + j
                if e:
                    for q in p5_copies(u, e):
                        q.wait_recv()
                    parts.append((rm5[u, e], rc5[u, e]))
            rows = [wide(v[0]) for v in parts]
            yi = wrap(y - i, NY)
            gq[y, c, u, yi, pl.ds(0, 32)] = ((rows[0] + rows[1]) + (rows[2] + rows[3])).astype(I16)
            code = (parts[0][1] + parts[1][1]) + (parts[2][1] + parts[3][1])
            gq[y, c, u, yi, pl.ds(32, 16)] = tail([code])
        begin([half_copy(u, c)])

    def rank_row(b, carry):
        ob = owner[b]
        total = jnp.int32(0)
        for e in range(NB):
            total = total + jnp.where((owner[e] == ob) & (e < b), 1, 0)
        rank[b] = total
        return carry

    def find(i, carry):
        target = lax.div(i, SLOTS) * NZ + z
        slot = lax.rem(i, SLOTS)
        found = jnp.int32(-1)
        for j in range(8):
            b = 4 * x + j if j < 4 else 16 + 4 * x + j - 4
            found = jnp.where((owner[b] == target) & (rank[b] == slot), j, found)
        local_j[i] = found
        return carry

    far(0)
    near(0)
    far(1)
    onward(0)
    near(1)
    onward(1)
    last(0)
    last(1)
    along_z(0)
    along_z(1)
    owner_copy.wait()
    lax.fori_loop(0, NB, rank_row, 0)
    lax.fori_loop(0, NX * SLOTS, find, 0)
    n_mine = jnp.int32(0)
    for b in range(NB):
        n_mine = n_mine + jnp.where(owner[b] == grp, 1, 0)
    pieces = [gather_z(u) for u in range(2)]
    route(0)
    route(1)
    collect(0)
    collect(1)
    g_square = jnp.sum(jnp.sum(pieces[0] * pieces[0] + pieces[1] * pieces[1], axis=0), axis=0, keepdims=True)

    def block_copies(slot, core, ssem, rsem, to):
        return [remote(gq.at[slot, core], gq.at[slot, core], ssem, rsem, to)]

    for k in (2, 1, 3):
        begin(block_copies(y, c, s_6.at[k - 1], r_6.at[k - 1], dev(dy=k)))
    stat_copy.wait()
    for u in range(2):
        open_half(y, c, u)
    for u in range(2):
        half_copy(u, oc).wait_recv()
        open_half(y, oc, u)

    def put_stats(slot, side, value):
        ns[slot, side] = jnp.where(n_mine > slot, value, stats[slot, side])

    def slot_stats(slot):
        for core in range(NC):
            for u in range(2):
                open_half(slot, core, u)
        g = gbuf[...].reshape(BS, BS)
        gp, gtp = split(g), split(g.T)
        put_stats(slot, 0, DECAY * stats[slot, 0] + dot3(gp, gtp))
        put_stats(slot, 1, DECAY * stats[slot, 1] + dot3(gtp, gp))

    g = gbuf[...].reshape(BS, BS)
    gt = g.T
    first, second = jnp.where(c == 0, g, gt), jnp.where(c == 0, gt, g)
    first_p, second_p = split(first), split(second)
    mat = DECAY * stats[y, c] + dot3(first_p, second_p)
    put_stats(y, c, mat)
    norm = jnp.sqrt(jnp.sum(jnp.sum(mat * mat, axis=0, keepdims=True), axis=1, keepdims=True))
    five = jnp.where(
        lax.broadcasted_iota(jnp.int32, (BS, BS), 0) == lax.broadcasted_iota(jnp.int32, (BS, BS), 1), 1.25, 0.0
    ).astype(F32)
    q0 = mat * (1.0 / norm)
    factor = five - 0.25 * q0
    xs[...] = factor * lax.rsqrt(jnp.sqrt(norm))

    def newton(i, carry):
        q = qs[...]
        fp = split(five - 0.25 * q)
        square = split(dot3(fp, fp))
        x_next = dot3(split(xs[...]), fp)
        qs[...] = dot3(split(dot3(square, square)), split(q))
        xs[...] = x_next
        return carry

    fp = split(factor)
    square = split(dot3(fp, fp))
    qs[...] = dot3(split(dot3(square, square)), split(q0))
    lax.fori_loop(0, ITERS - 3, newton, 0)
    q = qs[...]
    factor = five - 0.25 * q
    fp = split(factor)
    x5 = dot3(split(xs[...]), fp)
    square = split(dot3(fp, fp))
    fourth = dot3(square, square)
    xs[...] = 1.25 * x5 - 0.25 * dot3(split(fourth), split(dot3(split(q), split(x5))))

    root_copy = send(xs, xother, s_x, r_x, dev(dc=1))
    one_side = dot3(split(xs[...]), first_p)
    one_half = one_side.T[:, 128:]
    for k in (1, 2, 3):
        yk = wrap(y - k, NY)
        for q in block_copies(yk, c, s_6.at[k - 1], r_6.at[k - 1], dev(dy=k)):
            q.wait_recv()
        begin(block_copies(yk, c, s_7.at[k - 1], r_7.at[k - 1], dev(dc=1)))
    root_copy.wait_recv()
    other = xother[...]
    prec = dot3(
        split(jnp.where(c == 0, one_side, other)), split(jnp.where(c == 0, other[:, :128], one_half))
    ).reshape(32, 8, 128)
    p_square = jnp.sum(jnp.sum(prec * prec, axis=0), axis=0, keepdims=True)
    p_code = code_of(jnp.max(peak(prec), axis=0, keepdims=True))
    inverse = 1.0 / scale_of(p_code)
    end = jnp.concatenate([p_code] + sum_rows(g_square) + sum_rows(p_square) + [jnp.zeros((3, 128), F32)], axis=0)
    for i in range(NX * NZ):
        rows = (prec[i] * inverse + 12582912.0) - 12582912.0
        ma[i] = to16(jnp.concatenate([rows, end], axis=0))

    w = []
    for k in (4, 3, 5, 2, 6, 1, 7, 0):
        for j in (2, 1, 3, 0):
            if k or j:
                e = j * 8 + k
                w.append(send(ma.at[wrap(x + j, NX) * 8 + wrap(z + k, NZ)], rma.at[e], s_a.at[e], r_a.at[e], dev(dx=j, dz=k)))
    rma[0] = ma[grp]
    flush()
    put_stats(y, oc, DECAY * stats[y, oc] + dot3(second_p, first_p))

    def other_slot(k):
        yk = wrap(y - k, NY)
        for q in block_copies(yk, oc, s_7.at[k - 1], r_7.at[k - 1], dev(dc=1)):
            q.wait_recv()
        slot_stats(yk)

    def sums_of(end, at):
        return sums_from(end[at:at + 2]), sums_from(end[at + 2:at + 4])

    def add(pairs):
        while len(pairs) > 1:
            pairs = [(a[0] + b[0], a[1] + b[1]) for a, b in zip(pairs[::2], pairs[1::2])]
        return pairs[0]

    other_slot(1)
    for q in w:
        q.wait_recv()

    def pick(i, carry):
        pair = []
        for u in range(2):
            b = 2 * i + u
            o = owner[b]
            at = wrap(x - lax.div(o, NZ), NX) * 8 + wrap(z - lax.rem(o, NZ), NZ)
            pair.append(jnp.where(rank[b] == y, wide(rma[at]), jnp.zeros((16, 128), jnp.int32)))
            codes[pl.ds(lax.rem(b, 8), 1)] = pair[u][8:9].astype(F32)
        rows = jnp.concatenate([v[0:8] for v in pair], axis=0).astype(I16)
        my[lax.div(i, 4), pl.ds(pl.multiple_of(lax.rem(i, 4) * 16, 16), 16)] = rows
        return carry

    w = []
    for k in (2, 1, 3, 0):
        yy = wrap(y + k, NY)
        lax.fori_loop(4 * yy, 4 * yy + 4, pick, 0)
        my[yy, pl.ds(64, 16)] = tail([codes[...]])
        if k:
            w.append(send(my.at[yy], rmy.at[k], s_y.at[k], r_y.at[k], dev(dy=k)))
    g_sum, p_sum = add([sums_of(wide(rma[e]).astype(F32), 9) for e in range(NX * NZ)])
    flush()
    other_slot(2)
    for q in w:
        q.wait_recv()
    ends = [wide(v).astype(F32) for v in (my[y, pl.ds(64, 16)], rmy[1, pl.ds(64, 16)],
                                          rmy[2, pl.ds(64, 16)], rmy[3, pl.ds(64, 16)])]
    block_codes = (ends[0][0:8] + ends[1][0:8]) + (ends[2][0:8] + ends[3][0:8])
    fq[c, y, pl.ds(0, 64)] = (
        (wide(my[y, pl.ds(0, 64)]) + wide(rmy[1, pl.ds(0, 64)]))
        + (wide(rmy[2, pl.ds(0, 64)]) + wide(rmy[3, pl.ds(0, 64)]))
    ).astype(I16)
    fq[c, y, pl.ds(64, 16)] = tail([block_codes] + sum_rows(g_sum) + sum_rows(p_sum) + [jnp.zeros((4, 128), F32)])

    def ag_copy(core, yy, e, to):
        return remote(fq.at[core, yy], fq.at[core, yy], s_ag.at[e], r_ag.at[e], to)

    for k in (2, 1, 3, 0):
        for o in range(2):
            e = k * 2 + o
            if e:
                begin([ag_copy(c, y, e, dev(dy=k, dc=o))])
    other_slot(3)
    for k in range(NY):
        for o in range(2):
            e = k * 2 + o
            if e:
                ag_copy(wrap(c + o, 2), wrap(y - k, NY), e, dev(dy=k, dc=o)).wait_recv()
    g_sum, p_sum = add([sums_of(wide(fq[core, yy, pl.ds(64, 16)]).astype(F32), 8) for core in range(NC) for yy in range(NY)])
    ratio = jnp.sqrt(jnp.sum(g_sum, axis=1, keepdims=True) / jnp.sum(p_sum, axis=1, keepdims=True))
    ratio_ref[...] = jnp.broadcast_to(ratio, (1, 128))
    flush()


def hand_over(fq, ratio, ns_in, dir_out, ns_out, direction, sems):
    copies = []
    for i in range(SLOTS):
        for j in range(2):
            for half in range(2):
                at = (i, j, pl.ds(128 * half, 128))
                copies.append(pltpu.make_async_copy(ns_in.at[at], ns_out.at[at], sems.at[2 + len(copies)]))
    for q in copies:
        q.start()
    for half in range(2):
        for yy in (2 * half, 2 * half + 1):
            for h in range(NC):
                block_scales = scale_of(wide(fq[h, yy, pl.ds(64, 16)]).astype(F32)) * ratio[...]
                for i in range(8):
                    both = wide(fq[h, yy, pl.ds(16 * (i // 2), 16)]).astype(F32)
                    at = (yy * 8 + i) * 256 + h * 128
                    direction[:, pl.ds(at, 128)] = both[8 * (i % 2):8 * (i % 2) + 8] * block_scales[i:i + 1]
        at = (slice(None), pl.ds(4096 * half, 4096))
        copies.append(pltpu.make_async_copy(direction.at[at], dir_out.at[at], sems.at[half]))
        copies[-1].start()
    for q in copies:
        q.wait()


def local(grad_parts, stats, owner):
    grad = grad_parts.reshape(NY, NC, 32, 8192)
    vm, dma = pltpu.VMEM, pltpu.SemaphoreType.DMA
    t = (8, 128)
    scratch = [
        vm((SLOTS, 2, BS, BS), F32),
        vm((NY, 32, 8192), BF16), vm((NY, 32, 8192), BF16),
        vm((2, 2, 6, 272, 128), I16), vm((2, 2, 6, 272, 128), I16),
        vm((2, 2, 4, 4, 4) + t, F32),
        vm((2, 2, 4, 144, 128), I16), vm((2, 2, 4, 144, 128), I16),
        vm((2, 8, 4) + t, F32),
        vm((2, 8, 32, 128), I16), vm((2, 8, 32, 128), I16),
        vm((2, 8, 1, 128), F32), vm((2, 8, 1, 128), F32),
        vm((8, 32, 128), I16), vm((8, 32, 128), I16),
        vm((8, 1, 128), F32), vm((8, 1, 128), F32),
        vm((2, 16, 32, 128), I16), vm((2, 16, 32, 128), I16),
        vm((2, 16, 1, 128), F32), vm((2, 16, 1, 128), F32),
        vm((SLOTS, NC, 2, NY, 48, 128), I16),
        vm((NY, NC, 32, BS), F32),
        vm((8, 128), F32), vm((2, 4, 4) + t, F32),
        vm((BS, BS), F32), vm((BS, BS), F32), vm((BS, BS), F32),
        vm((32, 16, 128), I16), vm((32, 16, 128), I16),
        vm((NY, 80, 128), I16), vm((NY, 80, 128), I16),
        pltpu.SMEM((NB,), jnp.int32), pltpu.SMEM((NB,), jnp.int32), pltpu.SMEM((NX * SLOTS,), jnp.int32),
        dma, dma((10,)), dma, dma((10,)), dma((10,)), dma((2, 2, 6)), dma((2, 2, 6)),
        dma((2, 2, 4)), dma((2, 2, 4)), dma((2, 2, 8)), dma((2, 2, 8)), dma((2, 2, 7)), dma((2, 2, 7)),
        dma((2, 2, 16)), dma((2, 2, 16)),
        dma((2,)), dma((2,)), dma((3,)), dma((3,)), dma((3,)), dma((3,)), dma, dma,
        dma((32,)), dma((32,)), dma((4,)), dma((4,)), dma((8,)), dma((8,)),
    ]
    results = pl.pallas_call(
        kernel,
        out_shape=(pltpu.VMEM((NC, NY, 80, 128), I16), pltpu.VMEM((1, 128), F32), pltpu.VMEM((SLOTS, 2, BS, BS), F32)),
        in_specs=[
            pl.BlockSpec(memory_space=pltpu.HBM),
            pl.BlockSpec(memory_space=pltpu.HBM),
            pl.BlockSpec(memory_space=pltpu.HBM),
        ],
        out_specs=(pl.BlockSpec(memory_space=pltpu.VMEM),) * 3,
        scratch_shapes=scratch,
        compiler_params=pltpu.CompilerParams(
            collective_id=0, has_side_effects=True, vmem_limit_bytes=51 * 1024 * 1024
        ),
        cost_estimate=pl.CostEstimate(flops=4_000_000_000, bytes_accessed=9_000_000, transcendentals=0),
    )(*[pltpu.with_memory_space_constraint(v, pltpu.HBM) for v in (grad, stats, owner)])
    return pl.pallas_call(
        hand_over,
        out_shape=(
            jax.ShapeDtypeStruct((8, 8192), F32),
            jax.ShapeDtypeStruct((SLOTS, 2, BS, BS), F32),
        ),
        in_specs=[pl.BlockSpec(memory_space=pltpu.VMEM)] * 3,
        out_specs=(pl.BlockSpec(memory_space=pltpu.HBM), pl.BlockSpec(memory_space=pltpu.HBM)),
        scratch_shapes=[vm((8, 8192), F32), dma((2 + 4 * SLOTS,))],
    )(*[pltpu.with_memory_space_constraint(v, pltpu.VMEM) for v in results])


def solution(mesh):
    return jax.shard_map(
        local,
        mesh=mesh,
        in_specs=(P("rep", "grp", None, None), P("grp", None, None, None), P()),
        out_specs=(P("grp", None), P("grp", None, None, None)),
        check_vma=False,
    )
```
